32 devices in a mesh: dp: 4 (over y, x), latent: 8 (over z, core).
Axes of the slice: x: 2, y: 2, z: 4, core: 2. Of those that a mesh axis runs over, the one named last changes fastest.
Arguments:
- queries: bfloat16 [1024, 2048], P(('dp', 'latent')), may hold values from -32 to 32, as said below
- cache_keys: bfloat16 [32, 512, 1024], P(('dp', 'latent')), may hold values from -6 to 6
- cache_values: bfloat16 [32, 512, 1024], P(('dp', 'latent')), may hold values from -96 to 96
- positions: int32 [1024], P(('dp', 'latent')), may hold values from 224 to 511, as said below
- shuffle: int32 [1024], P(('dp', 'latent')), may hold values from 0 to 1023, as said below
- enc_weight: bfloat16 [2048, 16384], P(None, 'latent'), may hold values from -0.125 to 0.125
- enc_bias: float32 [16384], P('latent'), may hold values from -3 to 3
- dec_weight: bfloat16 [16384, 2048], P('latent'), may hold values from -0.046875 to 0.046875
- dec_bias: float32 [2048], replicated, may hold values from -3 to 3
Outputs:
- rebuilt: bfloat16 [1024, 2048], P(('dp', 'latent'))
- grad_enc: float32 [2048, 16384], P('dp', 'latent')
- grad_dec: float32 [16384, 2048], P('latent', 'dp')
The draws below stay inside these ranges and needn't reach their ends.
Inputs may be any that keep to these rules, and one draw needn't show every extreme that they name: `queries`: entries are finite; a few rows may be aligned with keys of their sequence. The rows of one sequence have consecutive positions ending at its length minus one; lengths lie between 256 and 512, and sequence 0 has length 512. A permutation of 0 to 1023. Row r and its place shuffle[r] lie in sequences r // 32 and shuffle[r] // 32 that are equal modulo 256 // 32; from each such sequence exactly 8 rows go to each such sequence.
All inputs are finite; a program needn't handle non-finite values.
Results may differ from the reference program's by a relative error of at most 0.012.
Values may be sent and summed in bfloat16 or wider, within the bound.
No kernel may reach another device: no remote copies, remote signals or barrier semaphores. Data moves between devices by JAX's collectives and lax.ppermute only.
A program may use at most 128 MiB of HBM per device.

```python
import math
import jax
import jax.numpy as jnp
from jax import lax

HEADS = 8
KV_HEADS = 4
HEAD_DIM = 256
LATENTS = 16384
Q_DEV = 32
CACHE = 512
D_ATT = 2048
SEQS = 32
ROWS = 1024
GROUP_ROWS = 256
PER_PEER = 8
N_DP = 4
N_LATENT = 8


def attention_draw(key):
    key_part = jax.random.fold_in(key, 101)
    query_part = jax.random.fold_in(key, 102)
    keys_arr = jnp.clip(jax.random.normal(key_part, (SEQS, CACHE, KV_HEADS * HEAD_DIM), jnp.float32), -6.0, 6.0)
    query_arr = jnp.clip(jax.random.normal(query_part, (ROWS, HEADS * HEAD_DIM), jnp.float32), -6.0, 6.0)
    return (query_arr, keys_arr)


def draw_queries(key, part):
    return attention_draw(key)[0].astype(jnp.bfloat16)


def draw_cache_keys(key, part):
    return attention_draw(key)[1].astype(jnp.bfloat16)


def draw_cache_values(key, part):
    value_part = jax.random.fold_in(key, 201)
    slot_part = jax.random.fold_in(key, 202)
    shape = (SEQS, CACHE, KV_HEADS * HEAD_DIM)
    seq_scale = 3.0 ** (jnp.arange(SEQS, dtype=jnp.float32) / max(SEQS - 1, 1))
    slot_scale = jnp.exp(jax.random.uniform(slot_part, (SEQS, CACHE, 1), jnp.float32, math.log(0.5), math.log(5.0)))
    base = jnp.clip(jax.random.normal(value_part, shape, jnp.float32), -6.0, 6.0)
    return (base * slot_scale * seq_scale[:, None, None]).astype(jnp.bfloat16)


def draw_positions(key, part):
    length_part = jax.random.fold_in(key, 301)
    lengths = jax.random.randint(length_part, (SEQS,), CACHE // 2, CACHE + 1)
    lengths = lengths.at[0].set(CACHE)
    offsets = jnp.arange(Q_DEV, dtype=jnp.int32)
    return (lengths[:, None] - Q_DEV + offsets[None, :]).reshape(ROWS).astype(jnp.int32)


def one_permutation(subkey):
    return jax.random.permutation(subkey, Q_DEV)


def draw_shuffle(key, part):
    rank_part = jax.random.fold_in(key, 401)
    place_part = jax.random.fold_in(key, 402)
    ranks = jax.vmap(one_permutation)(jax.random.split(rank_part, SEQS)).astype(jnp.int32)
    places = jax.vmap(one_permutation)(jax.random.split(place_part, SEQS)).astype(jnp.int32)
    device = jnp.arange(SEQS, dtype=jnp.int32)[:, None]
    source_dp = device // N_LATENT
    latent_index = device % N_LATENT
    target_dp = ranks // PER_PEER
    arrival = source_dp * PER_PEER + ranks % PER_PEER
    target_dev = target_dp * N_LATENT + latent_index
    slot = places[target_dev, arrival]
    return (target_dev * Q_DEV + slot).reshape(ROWS).astype(jnp.int32)


def level_of(key, extent, cuts, smallest, high):
    loudness, own = 1.0, jax.random.fold_in(key, 6)
    for axis_at, parts in cuts:
        heights = jnp.exp(jax.random.uniform(jax.random.fold_in(own, axis_at), (parts,), jnp.float32, smallest / len(cuts), high / len(cuts)))
        loudness = loudness * jnp.repeat(heights, extent[axis_at] // parts).reshape([-1 if axis == axis_at else 1 for axis in range(len(extent))])
    return loudness


def bell_draw(rng, shape, scale, bound, pieces=(), kind=jnp.bfloat16):
    drawn = scale * jax.random.normal(rng, shape, jnp.float32)
    if pieces:
        drawn = drawn * level_of(rng, shape, pieces, -0.22, 0.18)
    return jnp.clip(drawn, -bound, bound).astype(kind)


def setup_inputs(seed: int = 0) -> dict:
    key_of = jax.random.split(jax.random.key(seed), 10)
    return {
        "queries": draw_queries(jax.random.fold_in(key_of[9], 71), 0),
        "cache_keys": draw_cache_keys(jax.random.fold_in(key_of[9], 71), 0),
        "cache_values": draw_cache_values(jax.random.fold_in(key_of[9], 71), 0),
        "positions": draw_positions(jax.random.fold_in(key_of[9], 71), 0),
        "shuffle": draw_shuffle(jax.random.fold_in(key_of[9], 71), 0),
        "enc_weight": bell_draw(key_of[5], (D_ATT, LATENTS), D_ATT ** -0.5, 0.125, ((1, 8),)),
        "enc_bias": bell_draw(key_of[6], (LATENTS,), 0.5, 3.0, ((0, 8),), jnp.float32),
        "dec_weight": bell_draw(key_of[7], (LATENTS, D_ATT), LATENTS ** -0.5, 0.046875, ((0, 8),)),
        "dec_bias": bell_draw(key_of[8], (D_ATT,), 0.5, 3.0, (), jnp.float32),
    }


sharpness = 4.0
sparsity_weight = 1.0
epsilon = 1e-06

def attend(query_rows, key_rows, value_rows, position_rows):
    grouped = query_rows.reshape(Q_DEV, KV_HEADS, HEADS // KV_HEADS, HEAD_DIM).astype(jnp.float32)
    keys_local = key_rows.reshape(CACHE, KV_HEADS, HEAD_DIM).astype(jnp.float32)
    values_local = value_rows.reshape(CACHE, KV_HEADS, HEAD_DIM).astype(jnp.float32)
    scores = jnp.einsum('qgid,kgd->gqik', grouped, keys_local) * HEAD_DIM ** (-0.5)
    slot_index = jnp.arange(CACHE)
    visible = slot_index[None, None, None, :] <= position_rows[None, :, None, None]
    scores = jnp.where(visible, scores, -jnp.inf)
    highest = lax.optimization_barrier(jnp.max(scores, axis=-1, keepdims=True))
    weights = jnp.exp(scores - highest)
    weights = weights / lax.optimization_barrier(jnp.sum(weights, axis=-1, keepdims=True))
    attn_probs = lax.optimization_barrier(weights.astype(jnp.bfloat16)).astype(jnp.float32)
    head_mix = jnp.einsum('gqik,kgd->qgid', attn_probs, values_local)
    return head_mix.reshape(Q_DEV, D_ATT).astype(jnp.bfloat16)

def attend_packed(packed):
    return attend(packed[0], packed[1], packed[2], packed[3])

def reference(queries, cache_keys, cache_values, positions, shuffle, enc_weight, enc_bias, dec_weight, dec_bias):
    heads_out = lax.map(attend_packed, (queries.reshape(SEQS, Q_DEV, D_ATT), cache_keys, cache_values, positions.reshape(SEQS, Q_DEV)))
    heads_out = heads_out.reshape(ROWS, D_ATT).astype(jnp.float32)
    energy = jnp.sum(jnp.square(heads_out))
    norm_scale = 1.0 / jnp.sqrt(energy / (ROWS * D_ATT) + epsilon)
    normed = (heads_out * norm_scale).astype(jnp.bfloat16)
    inputs = jnp.zeros_like(normed).at[shuffle].set(normed)
    groups = inputs.reshape(N_DP, GROUP_ROWS, D_ATT)
    dec_float = dec_weight.astype(jnp.float32)
    dec_norms = jnp.sqrt(lax.optimization_barrier(jnp.sum(jnp.square(dec_float), axis=1)) + epsilon)

    def process_group(carry, gathered):
        enc_acc, dec_acc = carry
        preact = jnp.dot(gathered, enc_weight, preferred_element_type=jnp.float32) + enc_bias
        active = jax.nn.softplus(sharpness * preact) / sharpness
        coded = active.astype(jnp.bfloat16)
        rebuilt_full = jnp.dot(coded, dec_weight, preferred_element_type=jnp.float32) + dec_bias
        residual = rebuilt_full - gathered.astype(jnp.float32)
        residual_half = residual.astype(jnp.bfloat16)
        grad_active = 2.0 / ROWS * lax.dot_general(residual_half, dec_weight, (((1,), (1,)), ((), ())), preferred_element_type=jnp.float32)
        grad_active = grad_active + sparsity_weight / ROWS * dec_norms[None, :]
        grad_pre = (grad_active * jax.nn.sigmoid(sharpness * preact)).astype(jnp.bfloat16)
        enc_term = lax.dot_general(gathered, grad_pre, (((0,), (0,)), ((), ())), preferred_element_type=jnp.float32)
        column_sums = lax.optimization_barrier(jnp.sum(coded.astype(jnp.float32), axis=0))
        dec_term = 2.0 / ROWS * lax.dot_general(coded, residual_half, (((0,), (0,)), ((), ())), preferred_element_type=jnp.float32)
        dec_term = dec_term + sparsity_weight / ROWS * column_sums[:, None] * dec_float / dec_norms[:, None]
        enc_acc = enc_acc + enc_term.astype(jnp.bfloat16).astype(jnp.float32)
        dec_acc = dec_acc + dec_term.astype(jnp.bfloat16).astype(jnp.float32)
        return ((enc_acc, dec_acc), rebuilt_full.astype(jnp.bfloat16))
    start_carry = (jnp.zeros((D_ATT, LATENTS), jnp.float32), jnp.zeros((LATENTS, D_ATT), jnp.float32))
    final_carry, rebuilt = lax.scan(process_group, start_carry, groups)
    grad_enc, grad_dec = final_carry
    return (rebuilt.reshape(ROWS, D_ATT), grad_enc, grad_dec)
```

```python
import functools

import jax
import jax.numpy as jnp
from jax import lax
from jax.experimental import pallas as pl
from jax.experimental.pallas import tpu as pltpu
from jax.sharding import PartitionSpec as P

HEAD_DIM = 256


sharpness = 4.0
sparsity_weight = 1.0
epsilon = 1e-06


def attend(queries, cache_keys, cache_values, positions):
    rows_here = queries.shape[0]
    kv_heads = cache_keys.shape[-1] // HEAD_DIM
    grouped = queries.reshape(rows_here, kv_heads, -1, HEAD_DIM)
    keys_local = cache_keys[0].reshape(-1, kv_heads, HEAD_DIM)
    values_local = cache_values[0].reshape(-1, kv_heads, HEAD_DIM)
    scores = jnp.einsum(
        "qgid,kgd->gqik", grouped, keys_local, preferred_element_type=jnp.float32
    ) * HEAD_DIM ** (-0.5)
    slot_index = jnp.arange(keys_local.shape[0])
    visible = slot_index[None, None, None, :] <= positions[None, :, None, None]
    scores = jnp.where(visible, scores, -jnp.inf)
    highest = jnp.max(scores, axis=-1, keepdims=True)
    weights = jnp.exp(scores - highest)
    attn_probs = (weights / jnp.sum(weights, axis=-1, keepdims=True)).astype(jnp.bfloat16)
    head_mix = jnp.einsum(
        "gqik,kgd->qgid", attn_probs, values_local, preferred_element_type=jnp.float32
    )
    return head_mix.reshape(rows_here, -1).astype(jnp.bfloat16)


VMEM_BYTES = 40 * 1024 * 1024


def codes(scaled):
    decay = jnp.exp(-jnp.abs(scaled))
    inverse = 1.0 / ((1.0 + decay) * (2.0 + decay))
    ratio = decay * inverse * (1.0 + decay)
    square = ratio * ratio
    series = 1.0 / 13.0
    for odd in (11, 9, 7, 5, 3, 1):
        series = series * square + 1.0 / odd
    soft = jnp.maximum(scaled, 0.0) + 2.0 * ratio * series
    slope = jnp.where(scaled >= 0.0, 1.0, decay) * (2.0 + decay) * inverse
    return (soft * (1.0 / sharpness)).astype(jnp.bfloat16), slope.astype(jnp.bfloat16)


def encode_body(scale_ref, rows_ref, enc_ref, bias_ref, coded_ref, slope_ref):
    scale = scale_ref[0, 0] * sharpness
    product = jnp.dot(rows_ref[...], enc_ref[...], preferred_element_type=jnp.float32)
    coded, slope = codes(product * scale + bias_ref[...] * sharpness)
    coded_ref[...] = coded
    slope_ref[...] = slope


def rebuild_body(scale_ref, rows_ref, enc_ref, bias_ref, dec_ref, coded_ref, slope_ref, total_ref):
    encode_body(scale_ref, rows_ref, enc_ref, bias_ref, coded_ref, slope_ref)
    term = jnp.dot(coded_ref[...], dec_ref[...], preferred_element_type=jnp.float32)

    @pl.when(pl.program_id(0) == 0)
    def _():
        total_ref[...] = term

    @pl.when(pl.program_id(0) > 0)
    def _():
        total_ref[...] += term


def encode(scale, rows, enc_weight, bias, dec_weight=None):
    count, width = rows.shape
    latents = enc_weight.shape[1]
    tile = min(512, latents)
    flops = 2 * count * width * latents
    wide = jax.ShapeDtypeStruct((count, latents), jnp.bfloat16)
    wide_spec = pl.BlockSpec((count, tile), lambda j: (0, j))
    in_specs = [
        pl.BlockSpec(memory_space=pltpu.SMEM),
        pl.BlockSpec((count, width), lambda j: (0, 0)),
        pl.BlockSpec((width, tile), lambda j: (0, j)),
        pl.BlockSpec((1, tile), lambda j: (0, j)),
    ]
    args, outs, out_specs, body = [scale, rows, enc_weight, bias], [wide, wide], [wide_spec] * 2, encode_body
    if dec_weight is not None:
        body = rebuild_body
        args.append(dec_weight)
        in_specs.append(pl.BlockSpec((tile, width), lambda j: (j, 0)))
        outs.append(jax.ShapeDtypeStruct((count, width), jnp.float32))
        out_specs.append(pl.BlockSpec((count, width), lambda j: (0, 0)))
        flops *= 2
    return pl.pallas_call(
        body,
        grid=(latents // tile,),
        in_specs=in_specs,
        out_specs=out_specs,
        out_shape=outs,
        compiler_params=pltpu.CompilerParams(vmem_limit_bytes=VMEM_BYTES),
        cost_estimate=pl.CostEstimate(flops=flops, bytes_accessed=4 * width * latents, transcendentals=2 * count * latents),
    )(*args)


def slope_body(all_rows, residual_ref, dec_ref, norms_ref, slope_ref, out_ref):
    product = lax.dot_general(
        residual_ref[...], dec_ref[...], (((1,), (1,)), ((), ())), preferred_element_type=jnp.float32
    )
    grad = product * (2.0 / all_rows) + norms_ref[...] * (sparsity_weight / all_rows)
    out_ref[...] = (grad * slope_ref[...].astype(jnp.float32)).astype(jnp.bfloat16)


def pre_gradient(all_rows, residual, dec_weight, norms, slope):
    count, width = residual.shape
    latents = dec_weight.shape[0]
    tile = min(512, latents)
    wide_spec = pl.BlockSpec((count, tile), lambda j: (0, j))
    return pl.pallas_call(
        functools.partial(slope_body, all_rows),
        grid=(latents // tile,),
        in_specs=[
            pl.BlockSpec((count, width), lambda j: (0, 0)),
            pl.BlockSpec((tile, width), lambda j: (j, 0)),
            pl.BlockSpec((1, tile), lambda j: (0, j)),
            wide_spec,
        ],
        out_specs=wide_spec,
        out_shape=jax.ShapeDtypeStruct((count, latents), jnp.bfloat16),
        compiler_params=pltpu.CompilerParams(vmem_limit_bytes=VMEM_BYTES),
        cost_estimate=pl.CostEstimate(flops=2 * count * width * latents, bytes_accessed=2 * width * latents, transcendentals=0),
    )(residual, dec_weight, norms, slope)


def weight_body(groups, all_rows, scale_ref, norms_ref, dec_ref, *refs):
    rows, grads, coded, residual = (refs[i * groups : (i + 1) * groups] for i in range(4))
    enc_ref, out_ref = refs[4 * groups :]
    enc, dec, sums = 0.0, 0.0, 0.0
    ones = jnp.ones((rows[0].shape[0], 128), jnp.bfloat16)
    over_rows = (((0,), (0,)), ((), ()))
    for g in range(groups):
        enc = enc + lax.dot_general(rows[g][...], grads[g][...], over_rows, preferred_element_type=jnp.float32)
        dec = dec + lax.dot_general(coded[g][...], residual[g][...], over_rows, preferred_element_type=jnp.float32)
        sums = sums + lax.dot_general(coded[g][...], ones, over_rows, preferred_element_type=jnp.float32)
    enc_ref[...] = enc * scale_ref[0, 0]
    factor = sums[:, :1] / norms_ref[...] * (sparsity_weight / all_rows)
    out_ref[...] = dec * (2.0 / all_rows) + factor * dec_ref[...].astype(jnp.float32)


def weight_gradients(all_rows, scale, norms, dec_part, rows, grads, coded, residual):
    groups = len(rows)
    count, columns = rows[0].shape
    latents = dec_part.shape[0]
    tile = min(256, latents)
    narrow = [pl.BlockSpec((count, columns), lambda j: (0, 0))] * groups
    wide = [pl.BlockSpec((count, tile), lambda j: (0, j))] * groups
    return pl.pallas_call(
        functools.partial(weight_body, groups, all_rows),
        grid=(latents // tile,),
        in_specs=[
            pl.BlockSpec(memory_space=pltpu.SMEM),
            pl.BlockSpec((tile, 1), lambda j: (j, 0)),
            pl.BlockSpec((tile, columns), lambda j: (j, 0)),
            *narrow,
            *wide,
            *wide,
            *narrow,
        ],
        out_specs=[
            pl.BlockSpec((columns, tile), lambda j: (0, j)),
            pl.BlockSpec((tile, columns), lambda j: (j, 0)),
        ],
        out_shape=[
            jax.ShapeDtypeStruct((columns, latents), jnp.float32),
            jax.ShapeDtypeStruct((latents, columns), jnp.float32),
        ],
        compiler_params=pltpu.CompilerParams(vmem_limit_bytes=VMEM_BYTES),
        cost_estimate=pl.CostEstimate(flops=4 * groups * count * columns * latents, bytes_accessed=16 * columns * latents, transcendentals=0),
    )(scale, norms, dec_part, *rows, *grads, *coded, *residual)


def swap(x, axis, mask):
    size = lax.axis_size(axis)
    return lax.ppermute(x, axis, [(i, i ^ mask) for i in range(size)])


def spread(x, axis, masks):
    return [x] + [swap(x, axis, mask) for mask in masks]


def exchange_cores(x):
    return swap(x, "latent", 1)


def spread_columns_energy(x):
    latent_size = lax.axis_size("latent")
    data_size = lax.axis_size("dp")
    x = x + swap(x, "latent", 1)
    x = sum(spread(x, "dp", range(1, data_size)))
    return sum(spread(x, "latent", range(2, latent_size, 2)))


def place_rows(rows, shuffle):
    data_size = lax.axis_size("dp")
    latent_size = lax.axis_size("latent")
    own = lax.axis_index("dp")
    rows_here = rows.shape[0]
    per_peer = rows_here // data_size
    target = shuffle // (rows_here * latent_size)
    place = shuffle % rows_here
    index = jnp.arange(rows_here)
    same = (target[:, None] == target[None, :]) & (index[None, :] < index[:, None])
    rank = jnp.sum(same.astype(jnp.int32), axis=1)
    arrived, slots = [], []
    for mask in range(data_size):
        chosen = (target == (own ^ mask))[None, :] & (
            rank[None, :] == jnp.arange(per_peer)[:, None]
        )
        sent = jnp.dot(
            chosen.astype(jnp.bfloat16), rows, preferred_element_type=jnp.float32
        ).astype(jnp.bfloat16)
        slot = jnp.sum(jnp.where(chosen, place[None, :], 0), axis=1)
        if mask:
            sent = swap(sent, "dp", mask)
            slot = swap(slot, "dp", mask)
        arrived.append(sent)
        slots.append(slot)
    slots = jnp.concatenate(slots)
    pick = (slots[None, :] == index[:, None]).astype(jnp.bfloat16)
    return jnp.dot(
        pick, jnp.concatenate(arrived), preferred_element_type=jnp.float32
    ).astype(jnp.bfloat16)


def shards(
    queries,
    cache_keys,
    cache_values,
    positions,
    shuffle,
    enc_weight,
    enc_bias,
    dec_weight,
    dec_bias,
):
    rows_here = queries.shape[0]
    att_width = queries.shape[1]
    data_size = lax.axis_size("dp")
    latent_size = lax.axis_size("latent")
    all_rows = rows_here * data_size * latent_size
    columns_here = att_width // data_size
    half = rows_here * latent_size // 2
    z_masks = range(2, latent_size, 2)
    first_column = lax.axis_index("dp") * columns_here

    heads_out = attend(queries, cache_keys, cache_values, positions)
    energy = spread_columns_energy(
        jnp.sum(jnp.square(heads_out.astype(jnp.float32)), axis=0).reshape(-1, 128).sum(axis=0, keepdims=True)
    )
    norm_scale = lax.rsqrt(jnp.sum(energy) / (all_rows * att_width) + epsilon)

    def gather_groups(own_rows):
        mine = jnp.concatenate(spread(own_rows, "latent", z_masks))
        halves = spread(mine, "dp", range(1, data_size))
        return [jnp.concatenate([h, exchange_cores(h)]) for h in halves]

    heads = gather_groups(heads_out)
    dec_float = dec_weight.astype(jnp.float32)
    dec_norms = jnp.sqrt(jnp.sum(jnp.square(dec_float), axis=1) + epsilon)

    scale = norm_scale.reshape(1, 1)
    bias = enc_bias[None, :]
    coded, slopes = [None] * data_size, [None] * data_size
    coded[0], slopes[0], partial_value = encode(scale, heads[0], enc_weight, bias, dec_weight)
    for g in range(1, data_size):
        coded[g], slopes[g] = encode(scale, heads[g], enc_weight, bias)
    paired = partial_value[:half] + exchange_cores(partial_value[half:])
    summed = paired[:rows_here]
    for slot, mask in enumerate(z_masks):
        summed = summed + swap(
            paired[(slot + 1) * rows_here : (slot + 2) * rows_here], "latent", mask
        )
    rebuilt_own = summed + dec_bias[None, :]
    inputs_own = (heads_out.astype(jnp.float32) * norm_scale).astype(jnp.bfloat16)
    residual_own = (rebuilt_own - inputs_own.astype(jnp.float32)).astype(jnp.bfloat16)
    residuals = gather_groups(residual_own)
    rebuilt = place_rows(rebuilt_own.astype(jnp.bfloat16), shuffle)

    def part(x):
        return lax.dynamic_slice_in_dim(x, first_column, columns_here, 1)

    grads = [
        pre_gradient(all_rows, residuals[g], dec_weight, dec_norms[None, :], slopes[g])
        for g in range(data_size)
    ]
    grad_enc, grad_dec = weight_gradients(
        all_rows,
        scale,
        dec_norms[:, None],
        part(dec_weight),
        [part(x) for x in heads],
        grads,
        coded,
        [part(x) for x in residuals],
    )
    return (rebuilt, grad_enc, grad_dec)


def solution(mesh):
    in_specs = (
        P(("dp", "latent"), None),
        P(("dp", "latent"), None, None),
        P(("dp", "latent"), None, None),
        P(("dp", "latent")),
        P(("dp", "latent")),
        P(None, "latent"),
        P("latent"),
        P("latent", None),
        P(),
    )
    out_specs = (P(("dp", "latent"), None), P("dp", "latent"), P("latent", "dp"))
    return jax.shard_map(shards, mesh=mesh, in_specs=in_specs, out_specs=out_specs, check_vma=False)
```

```python
import functools

import jax
import jax.numpy as jnp
from jax import lax
from jax.experimental import pallas as pl
from jax.experimental.pallas import tpu as pltpu
from jax.sharding import PartitionSpec as P

HEAD_DIM = 256


sharpness = 4.0
sparsity_weight = 1.0
epsilon = 1e-06

MIB = 1024 * 1024
LOG2E = 1.4426950408889634
IN_VMEM = pl.BlockSpec(memory_space=pltpu.VMEM)
IN_HBM = pl.BlockSpec(memory_space=pltpu.HBM)
IN_SMEM = pl.BlockSpec(memory_space=pltpu.SMEM)


def kernel_call(body, args, specs, outs, scratch=(), out_specs=None, flops=0, limit=24):
    return pl.pallas_call(
        body,
        in_specs=specs,
        out_specs=out_specs or [IN_VMEM] * len(outs),
        out_shape=outs,
        scratch_shapes=list(scratch),
        compiler_params=pltpu.CompilerParams(vmem_limit_bytes=limit * MIB),
        cost_estimate=pl.CostEstimate(flops=flops, bytes_accessed=0, transcendentals=0),
    )(*args)


def held(x):
    return pltpu.with_memory_space_constraint(x, pltpu.VMEM)


def half_array(*shape):
    return jax.ShapeDtypeStruct(shape, jnp.bfloat16)


def float_array(*shape):
    return jax.ShapeDtypeStruct(shape, jnp.float32)


def attend_body(
    kv_heads, parts, positions_ref, queries, keys, values, enc, heads_ref, energy_ref, enc_ref, q, k, v, sems, enc_sems
):
    rows, width = q.shape
    per_head = width // kv_heads // HEAD_DIM
    whole = pltpu.make_async_copy(queries, q, sems.at[2 * kv_heads])
    whole.start()
    copies = []
    for g in range(kv_heads):
        here = pl.ds(g * HEAD_DIM, HEAD_DIM)
        copies.append(pltpu.make_async_copy(keys.at[0, :, here], k.at[:, here], sems.at[2 * g]))
        copies.append(pltpu.make_async_copy(values.at[0, :, here], v.at[:, here], sems.at[2 * g + 1]))
    size = enc.shape[0] // parts
    weights = []
    for part in range(parts):
        here = pl.ds(part * size, size)
        weights.append(pltpu.make_async_copy(enc.at[here], enc_ref.at[here], enc_sems.at[part]))
    for copy in copies + weights:
        copy.start()
    whole.wait()
    shape = (rows, keys.shape[1])
    row_index = lax.broadcasted_iota(jnp.int32, shape, 0)
    visible = lax.broadcasted_iota(jnp.int32, shape, 1) <= positions_ref[0] + row_index
    visible = jnp.concatenate([visible] * per_head, axis=0)
    energy = jnp.zeros((1, 128), jnp.float32)
    for g in range(kv_heads):
        heads = [slice((g * per_head + i) * HEAD_DIM, (g * per_head + i + 1) * HEAD_DIM) for i in range(per_head)]
        grouped = jnp.concatenate([q[:, head] for head in heads], axis=0)
        here = slice(g * HEAD_DIM, (g + 1) * HEAD_DIM)
        copies[2 * g].wait()
        scores = lax.dot_general(
            grouped, k[:, here], (((1,), (1,)), ((), ())), preferred_element_type=jnp.float32
        ) * HEAD_DIM ** (-0.5)
        scores = jnp.where(visible, scores, -jnp.inf)
        weight = jnp.exp(scores - jnp.max(scores, axis=1, keepdims=True))
        probs = (weight / jnp.sum(weight, axis=1, keepdims=True)).astype(jnp.bfloat16)
        copies[2 * g + 1].wait()
        mix = jnp.dot(probs, v[:, here], preferred_element_type=jnp.float32).astype(jnp.bfloat16)
        for i, head in enumerate(heads):
            part = mix[i * rows : (i + 1) * rows]
            heads_ref[:, head] = part
            square = jnp.sum(jnp.square(part.astype(jnp.float32)), axis=0, keepdims=True)
            for lane in range(0, HEAD_DIM, 128):
                energy = energy + square[:, lane : lane + 128]
    energy_ref[...] = energy
    for copy in weights:
        copy.wait()


def attend(queries, cache_keys, cache_values, positions, enc, parts=8):
    rows, width = queries.shape
    slots, kv_width = cache_keys.shape[1:]
    kv_heads = kv_width // HEAD_DIM
    hbm = [pltpu.with_memory_space_constraint(x, pltpu.HBM) for x in (queries, cache_keys, cache_values, enc)]
    return kernel_call(
        functools.partial(attend_body, kv_heads, parts),
        [positions, *hbm],
        [IN_SMEM] + [IN_HBM] * 4,
        [half_array(rows, width), float_array(1, 128), pltpu.VMEM(enc.shape, enc.dtype)],
        [
            pltpu.VMEM((rows, width), jnp.bfloat16),
            pltpu.VMEM((slots, kv_width), jnp.bfloat16),
            pltpu.VMEM((slots, kv_width), jnp.bfloat16),
            pltpu.SemaphoreType.DMA((2 * kv_heads + 1,)),
            pltpu.SemaphoreType.DMA((parts,)),
        ],
        flops=4 * rows * slots * width,
    )


def norms_body(block, dec_ref, column_ref, row_ref):
    for first in range(0, dec_ref.shape[0], block):
        here = slice(first, first + block)
        square = jnp.square(dec_ref[here, :].astype(jnp.float32))
        norms = jnp.sqrt(jnp.sum(square, axis=1, keepdims=True) + epsilon)
        column_ref[here, :] = norms
        row_ref[:, here] = jnp.broadcast_to(norms, (block, 128)).T[:1]


def decoder_norms(dec):
    latents = dec.shape[0]
    return kernel_call(
        functools.partial(norms_body, 256),
        [held(dec)],
        [IN_VMEM],
        [float_array(latents, 1), float_array(1, latents)],
    )


def codes(scaled):
    decay = jnp.exp2(-jnp.abs(scaled))
    small = decay * (LOG2E - (0.5 * LOG2E) * decay)
    soft = jnp.maximum(scaled, 0.0) + jnp.where(decay < 1e-3, small, jnp.log2(1.0 + decay))
    slope = jnp.exp2(scaled - soft)
    return soft * (1.0 / (sharpness * LOG2E)), slope.astype(jnp.bfloat16)


def norm_scale(energy_ref, entries):
    return lax.rsqrt(jnp.sum(energy_ref[...], axis=1, keepdims=True) / entries + epsilon)


def add_body(a_ref, b_ref, sum_ref):
    sum_ref[...] = a_ref[...] + b_ref[...]


def add(a, b):
    return kernel_call(add_body, [a, b], [IN_VMEM] * 2, [float_array(*a.shape)], limit=4)[0]


def join_body(*refs):
    join(refs[:-1], refs[-1])


def joined(*pieces):
    count = sum(piece.shape[0] for piece in pieces)
    out = [half_array(count, pieces[0].shape[1])]
    return kernel_call(join_body, pieces, [IN_VMEM] * len(pieces), out, limit=4)[0]


def add_split_body(a_ref, b_ref, keep_ref, send_ref):
    half = keep_ref.shape[0]
    keep_ref[...] = a_ref[:half] + b_ref[:half].astype(jnp.float32)
    send_ref[...] = (a_ref[half:] + b_ref[half:].astype(jnp.float32)).astype(jnp.bfloat16)


def add_split(a, b):
    half, width = a.shape[0] // 2, a.shape[1]
    outs = [float_array(half, width), half_array(half, width)]
    return kernel_call(add_split_body, [a, b], [IN_VMEM] * 2, outs, limit=4)


def residual_body(entries, a_ref, b_ref, bias_ref, heads_ref, energy_ref, rebuilt_ref, residual_ref):
    rebuilt = a_ref[...] + b_ref[...].astype(jnp.float32) + bias_ref[...]
    inputs = (heads_ref[...].astype(jnp.float32) * norm_scale(energy_ref, entries)).astype(jnp.bfloat16)
    rebuilt_ref[...] = rebuilt.astype(jnp.bfloat16)
    residual_ref[...] = (rebuilt - inputs.astype(jnp.float32)).astype(jnp.bfloat16)


def own_residual(entries, *args):
    shape = args[0].shape
    body = functools.partial(residual_body, entries)
    return kernel_call(body, args, [IN_VMEM] * 5, [half_array(*shape), half_array(*shape)], limit=4)


def own_columns(x, own_ref, columns):
    return x[:, pl.ds(pl.multiple_of(own_ref[0] * columns, 128), columns)]


def join(pieces, rows):
    start = 0
    for piece in pieces:
        rows[start : start + piece.shape[0]] = piece[...]
        start += piece.shape[0]


def encode_body(count, tile, entries, energy_ref, own_ref, enc_ref, bias_ref, *refs):
    pieces, (codes_ref, slope_ref, part_ref), (rows, *rest) = refs[:count], refs[count : count + 3], refs[count + 3 :]
    if rest:
        dec_hbm, keep_ref, send_ref, dec_ref, rows, coded_ref, sems = rows, *rest
        parts = sems.shape[0]
        size = dec_hbm.shape[0] // parts
        copies = []
        for part in range(parts):
            here = pl.ds(part * size, size)
            copies.append(pltpu.make_async_copy(dec_hbm.at[here], dec_ref.at[here], sems.at[part]))
        for copy in copies:
            copy.start()
    join(pieces, rows)
    factor = sharpness * LOG2E
    scale = norm_scale(energy_ref, entries) * factor
    for first in range(0, enc_ref.shape[1], tile):
        here = slice(first, first + tile)
        product = jnp.dot(rows[...], enc_ref[:, here], preferred_element_type=jnp.float32)
        coded, slope = codes(product * scale + bias_ref[:, here] * factor)
        codes_ref[here, :] = coded.T.astype(jnp.bfloat16)
        slope_ref[:, here] = slope
        if rest:
            coded_ref[:, here] = coded.astype(jnp.bfloat16)
    part = own_columns(rows, own_ref, part_ref.shape[0])
    part_ref[...] = part.astype(jnp.float32).T.astype(jnp.bfloat16)
    if rest:
        half = keep_ref.shape[0]
        for copy in copies:
            copy.wait()
        for first in range(0, dec_ref.shape[1], tile):
            here = slice(first, first + tile)
            total = jnp.dot(coded_ref[...], dec_ref[:, here], preferred_element_type=jnp.float32)
            keep_ref[:, here] = total[:half]
            send_ref[:, here] = total[half:]


def encode(entries, energy, own, enc, bias, pieces, columns):
    width, latents = enc.shape
    count = sum(piece.shape[0] for piece in pieces)
    return kernel_call(
        functools.partial(encode_body, len(pieces), min(512, latents), entries),
        [energy, own, held(enc), bias, *pieces],
        [IN_VMEM, IN_SMEM] + [IN_VMEM] * (2 + len(pieces)),
        [half_array(latents, count), half_array(count, latents), half_array(columns, count)],
        [pltpu.VMEM((count, width), jnp.bfloat16)],
        flops=2 * count * width * latents,
    )


def rebuild_body(count, tile, entries, energy_ref, own_ref, enc_ref, bias_ref, dec_hbm, *refs):
    pieces, outs, scratch = refs[:count], refs[count : count + 6], refs[count + 6 :]
    encode_body(
        count, tile, entries, energy_ref, own_ref, enc_ref, bias_ref, *pieces, *outs[:3], dec_hbm, *outs[3:], *scratch
    )


def encode_and_rebuild(entries, energy, own, enc, bias, dec, pieces, columns):
    width, latents = enc.shape
    count = sum(piece.shape[0] for piece in pieces)
    return kernel_call(
        functools.partial(rebuild_body, len(pieces), min(512, latents), entries),
        [energy, own, held(enc), bias, pltpu.with_memory_space_constraint(dec, pltpu.HBM), *pieces],
        [IN_VMEM, IN_SMEM, IN_VMEM, IN_VMEM, IN_HBM] + [IN_VMEM] * len(pieces),
        [
            half_array(latents, count),
            half_array(count, latents),
            half_array(columns, count),
            float_array(count // 2, width),
            float_array(count // 2, width),
            pltpu.VMEM(dec.shape, dec.dtype),
        ],
        [
            pltpu.VMEM((count, width), jnp.bfloat16),
            pltpu.VMEM((count, latents), jnp.bfloat16),
            pltpu.SemaphoreType.DMA((8,)),
        ],
        flops=4 * count * width * latents,
    )


def slope_body(count, tile, all_rows, own_ref, dec_ref, norms_ref, slope_ref, *refs):
    pieces, (grad_ref, part_ref, rows) = refs[:count], refs[count:]
    join(pieces, rows)
    for first in range(0, dec_ref.shape[0], tile):
        here = slice(first, first + tile)
        product = lax.dot_general(
            rows[...], dec_ref[here, :], (((1,), (1,)), ((), ())), preferred_element_type=jnp.float32
        )
        grad = product * (2.0 / all_rows) + norms_ref[:, here] * (sparsity_weight / all_rows)
        grad_ref[:, here] = (grad * slope_ref[:, here].astype(jnp.float32)).astype(jnp.bfloat16)
    part_ref[...] = own_columns(rows, own_ref, part_ref.shape[1])


def pre_gradient(all_rows, own, dec, norms, slope, pieces, columns):
    latents, width = dec.shape
    count = sum(piece.shape[0] for piece in pieces)
    return kernel_call(
        functools.partial(slope_body, len(pieces), min(512, latents), all_rows),
        [own, held(dec), norms, slope, *pieces],
        [IN_SMEM] + [IN_VMEM] * (3 + len(pieces)),
        [half_array(count, latents), half_array(count, columns)],
        [pltpu.VMEM((count, width), jnp.bfloat16)],
        flops=2 * count * width * latents,
    )


def weight_body(groups, tile, all_rows, entries, energy_ref, own_ref, norms_ref, dec_ref, *refs):
    rows, grads, coded, residual = (refs[i * groups : (i + 1) * groups] for i in range(4))
    enc_out, dec_out, enc_buffer, dec_buffer, sems = refs[4 * groups :]
    columns = dec_buffer.shape[2]
    steps = dec_ref.shape[0] // tile
    scale = norm_scale(energy_ref, entries)

    def copies(step):
        slot, here = step % 2, pl.ds(step * tile, tile)
        return (
            pltpu.make_async_copy(enc_buffer.at[slot], enc_out.at[:, here], sems.at[slot, 0]),
            pltpu.make_async_copy(dec_buffer.at[slot], dec_out.at[here], sems.at[slot, 1]),
        )

    for step in range(steps):
        if step >= 2:
            for copy in copies(step - 2):
                copy.wait()
        here = slice(step * tile, (step + 1) * tile)
        enc, dec, sums = 0.0, 0.0, 0.0
        for g in range(groups):
            enc = enc + jnp.dot(rows[g][...], grads[g][:, here], preferred_element_type=jnp.float32)
            dec = dec + jnp.dot(coded[g][here, :], residual[g][...], preferred_element_type=jnp.float32)
            sums = sums + jnp.sum(coded[g][here, :].astype(jnp.float32), axis=1, keepdims=True)
        enc_buffer[step % 2] = enc * scale
        part = own_columns(dec_ref.at[here, :], own_ref, columns).astype(jnp.float32)
        factor = sums / norms_ref[here, :] * (sparsity_weight / all_rows)
        dec_buffer[step % 2] = dec * (2.0 / all_rows) + factor * part
        for copy in copies(step):
            copy.start()
    for step in range(max(steps - 2, 0), steps):
        for copy in copies(step):
            copy.wait()


def weight_gradients(all_rows, entries, energy, own, norms, dec, rows, grads, coded, residual):
    columns = rows[0].shape[0]
    latents = dec.shape[0]
    count = sum(x.shape[0] for x in grads)
    tile = min(512, latents)
    args = [norms, held(dec), *rows, *grads, *coded, *residual]
    return kernel_call(
        functools.partial(weight_body, len(rows), tile, all_rows, entries),
        [energy, own, *args],
        [IN_VMEM, IN_SMEM] + [IN_VMEM] * len(args),
        [pltpu.HBM((columns, latents), jnp.float32), pltpu.HBM((latents, columns), jnp.float32)],
        [
            pltpu.VMEM((2, columns, tile), jnp.float32),
            pltpu.VMEM((2, tile, columns), jnp.float32),
            pltpu.SemaphoreType.DMA((2, 2)),
        ],
        [IN_HBM, IN_HBM],
        flops=4 * count * columns * latents,
    )


def bits(size):
    found, bit = [], 1
    while bit < size:
        found.append(bit)
        bit *= 2
    return found


def swap(x, even, odd=None):
    count = lax.axis_size("dp") * lax.axis_size("latent")
    odd = even if odd is None else odd
    return lax.ppermute(
        x, ("dp", "latent"), [(i, i ^ (odd if i & 1 else even)) for i in range(count)]
    )


def line_steps():
    steps = bits(lax.axis_size("latent"))[1:]
    return list(zip(steps[::-1], steps, strict=True))


def plane_steps():
    latent_size = lax.axis_size("latent")
    steps = [bit * latent_size for bit in bits(lax.axis_size("dp"))]
    return list(zip(steps, steps[::-1], strict=True))


def after(value, *done):
    return lax.optimization_barrier((value, *done))[0]


def after(value, *done):
    return lax.optimization_barrier((value, *done))[0]


def send_body(group_bits, own_ref, shuffle_ref, rows_ref, *outs):
    count, width = rows_ref.shape
    per_peer = outs[0].shape[0]
    goes_to = lax.shift_right_logical(shuffle_ref[...], group_bits) ^ own_ref[0]
    slot = shuffle_ref[...] & (count - 1)
    over_lanes = (((1,), (1,)), ((), ()))
    sublane = lax.broadcasted_iota(jnp.int32, (count, count), 0)
    lane = lax.broadcasted_iota(jnp.int32, (count, count), 1)
    peer_row = jnp.broadcast_to(goes_to, (count, count)).astype(jnp.float32)
    one_hot = (sublane == lane).astype(jnp.bfloat16)
    peer_column = lax.dot_general(
        one_hot, peer_row.astype(jnp.bfloat16), over_lanes, preferred_element_type=jnp.float32
    )
    before = (peer_column == peer_row) & (sublane < lane)
    rank = jnp.sum(before.astype(jnp.float32), axis=0, keepdims=True)
    order = goes_to.astype(jnp.float32) * per_peer + rank
    pick = (order == sublane.astype(jnp.float32)).astype(jnp.bfloat16)
    rows = jnp.dot(pick, rows_ref[...], preferred_element_type=jnp.float32)
    slot_rows = jnp.broadcast_to(slot, (128, count)).astype(jnp.float32).astype(jnp.bfloat16)
    slots = lax.dot_general(pick, slot_rows, over_lanes, preferred_element_type=jnp.float32)
    for peer, out in enumerate(outs):
        here = slice(peer * per_peer, (peer + 1) * per_peer)
        out[:, :width] = rows[here]
        out[:, width:] = slots[here]


def place_body(*refs):
    *pieces, out_ref, rows = refs
    join(pieces, rows)
    width = out_ref.shape[1]
    index = lax.broadcasted_iota(jnp.int32, (rows.shape[0], rows.shape[0]), 1).astype(jnp.float32)
    pick = (rows[:, width : width + 1] == index).astype(jnp.bfloat16)
    out_ref[...] = lax.dot_general(
        pick, rows[:, :width].astype(jnp.bfloat16), (((0,), (0,)), ((), ())), preferred_element_type=jnp.float32
    ).astype(jnp.bfloat16)


def send_rows(own, rows, shuffle):
    data_size = lax.axis_size("dp")
    latent_size = lax.axis_size("latent")
    count, width = rows.shape
    out = float_array(count // data_size, width + 128)
    body = functools.partial(send_body, len(bits(count * latent_size)))
    specs = [IN_SMEM, IN_VMEM, IN_VMEM]
    sent = kernel_call(body, [own, shuffle, rows], specs, [out] * data_size, limit=4)
    return [swap(x, peer * latent_size) if peer else x for peer, x in enumerate(sent)]


def place_rows(arrived, count, width):
    scratch = [pltpu.VMEM((count, width + 128), jnp.float32)]
    specs = [IN_VMEM] * len(arrived)
    return kernel_call(place_body, arrived, specs, [half_array(count, width)], scratch, limit=4)[0]


def shards(
    queries,
    cache_keys,
    cache_values,
    positions,
    shuffle,
    enc_weight,
    enc_bias,
    dec_weight,
    dec_bias,
):
    rows_here = queries.shape[0]
    att_width = queries.shape[1]
    data_size = lax.axis_size("dp")
    latent_size = lax.axis_size("latent")
    all_rows = rows_here * data_size * latent_size
    columns = att_width // data_size
    entries = all_rows * att_width
    core = (1, 1)
    line, plane = line_steps(), plane_steps()
    own = lax.axis_index("dp").astype(jnp.int32).reshape(1)
    bias, out_bias, places, own = lax.optimization_barrier(
        (enc_bias[None, :], dec_bias[None, :], shuffle[None, :], own)
    )
    heads_out, energy, enc = attend(queries, cache_keys, cache_values, positions, after(enc_weight, bias, out_bias, places, own))

    small_steps = plane + [core] + line
    rows = heads_out
    for number, mask in enumerate(line):
        arrived = swap(rows, *mask)
        count = len(plane) if number == 0 else 1
        if number == len(line) - 1:
            count = len(small_steps)
        for small in small_steps[:count]:
            energy = add(energy, swap(energy, *small))
        small_steps = small_steps[count:]
        rows = joined(rows, after(arrived, energy))

    pieces = [rows, swap(rows, *plane[0])]
    group = [rows, swap(rows, *core)]
    *first_set, keep, send, dec = encode_and_rebuild(entries, energy, own, enc, bias, dec_weight, group, columns)
    encoded = [first_set]

    def cut(part, largest=512):
        return [part[i : i + largest] for i in range(0, part.shape[0], largest)]

    def encode_next(parts, now):
        parts = [after(part, now) for part in parts]
        encoded.append(encode(entries, energy, own, enc, bias, parts, columns))
        return encoded[-1][0]

    total, sent = add_split(keep, swap(send, *core))
    for number, mask in enumerate(line[::-1]):
        arrived = swap(sent, *mask)
        if number == 0:
            for step in plane[1:]:
                pieces = [after(piece, sent) for piece in pieces]
                pieces.append(swap(joined(*pieces), *step))
            second = [pieces[1], swap(pieces[1], *core)]
        if number == len(line) - 1:
            arrived = after(arrived, encode_next(second, sent))
        else:
            total, sent = add_split(total, arrived)
    rebuilt_own, residual_own = own_residual(entries, total, arrived, out_bias, heads_out, energy)

    rows = residual_own
    for number, mask in enumerate(line):
        arrived = swap(rows, *mask)
        if number == 0:
            norms_column, norms_row = decoder_norms(after(dec, rows))
            arrived = after(arrived, norms_row)
            far = [after(piece, rows) for piece in pieces[2:]]
            far = [part for piece in far for part in (piece, swap(piece, *core))]
        if number == len(line) - 1:
            done = [encode_next([part], rows) for piece in far for part in cut(piece)]
            arrived = after(arrived, *done)
        rows = joined(rows, arrived)
    grads = []

    def pre(parts, now):
        slope = encoded[len(grads)][1]
        parts = [after(part, now) for part in parts]
        grads.append(pre_gradient(all_rows, own, dec, norms_row, slope, parts, columns))
        return grads[-1][0]

    group = [rows, swap(rows, *core)]
    pieces = [rows]
    for number, mask in enumerate(plane):
        sent = pieces[0] if number == 0 else joined(*pieces)
        arrived = swap(sent, *mask)
        if number == 0:
            moved = send_rows(own, after(rebuilt_own, sent), places)
            arrived = after(arrived, pre(group, sent))
        elif number == 1:
            arrived = after(arrived, pre([pieces[1], swap(pieces[1], *core)], sent))
        pieces.append(arrived)
    far = [part for piece in pieces[2:] for part in (piece, swap(piece, *core))]
    for piece in far:
        for part in cut(piece):
            last = pre([part], pieces[-1])
    moved = [after(part, last) for part in moved]
    rebuilt = place_rows(moved, rows_here, att_width)
    grad_enc, grad_dec = weight_gradients(
        all_rows,
        entries,
        energy,
        own,
        norms_column,
        dec,
        [x[2] for x in encoded],
        [x[0] for x in grads],
        [x[0] for x in encoded],
        [x[1] for x in grads],
    )
    return (rebuilt, grad_enc, grad_dec)


def solution(mesh):
    in_specs = (
        P(("dp", "latent"), None),
        P(("dp", "latent"), None, None),
        P(("dp", "latent"), None, None),
        P(("dp", "latent")),
        P(("dp", "latent")),
        P(None, "latent"),
        P("latent"),
        P("latent", None),
        P(),
    )
    out_specs = (P(("dp", "latent"), None), P("dp", "latent"), P("latent", "dp"))
    return jax.shard_map(shards, mesh=mesh, in_specs=in_specs, out_specs=out_specs, check_vma=False)
```

```python
import functools

import jax
import jax.numpy as jnp
from jax import lax
from jax.experimental import pallas as pl
from jax.experimental.pallas import tpu as pltpu
from jax.sharding import PartitionSpec as P

HEAD_DIM = 256


sharpness = 4.0
sparsity_weight = 1.0
epsilon = 1e-06

MIB = 1024 * 1024
LOG2E = 1.4426950408889634
IN_VMEM = pl.BlockSpec(memory_space=pltpu.VMEM)
IN_HBM = pl.BlockSpec(memory_space=pltpu.HBM)
IN_SMEM = pl.BlockSpec(memory_space=pltpu.SMEM)


def kernel_call(body, args, specs, outs, scratch=(), out_specs=None, flops=0, limit=12):
    return pl.pallas_call(
        body,
        in_specs=specs,
        out_specs=out_specs or [IN_VMEM] * len(outs),
        out_shape=outs,
        scratch_shapes=list(scratch),
        compiler_params=pltpu.CompilerParams(vmem_limit_bytes=limit * MIB),
        cost_estimate=pl.CostEstimate(flops=flops, bytes_accessed=0, transcendentals=0),
    )(*args)


def held(x):
    return pltpu.with_memory_space_constraint(x, pltpu.VMEM)


def half_array(*shape):
    return jax.ShapeDtypeStruct(shape, jnp.bfloat16)


def float_array(*shape):
    return jax.ShapeDtypeStruct(shape, jnp.float32)


def attend_body(
    kv_heads, parts, positions_ref, queries, keys, values, enc, heads_ref, energy_ref, enc_ref, q, k, v, sems, enc_sems
):
    rows, width = q.shape
    per_head = width // kv_heads // HEAD_DIM
    whole = pltpu.make_async_copy(queries, q, sems.at[2 * kv_heads])
    whole.start()
    copies = []
    for g in range(kv_heads):
        here = pl.ds(g * HEAD_DIM, HEAD_DIM)
        copies.append(pltpu.make_async_copy(keys.at[0, :, here], k.at[:, here], sems.at[2 * g]))
        copies.append(pltpu.make_async_copy(values.at[0, :, here], v.at[:, here], sems.at[2 * g + 1]))
    size = enc.shape[0] // parts
    weights = []
    for part in range(parts):
        here = pl.ds(part * size, size)
        weights.append(pltpu.make_async_copy(enc.at[here], enc_ref.at[here], enc_sems.at[part]))
    for copy in copies + weights:
        copy.start()
    whole.wait()
    shape = (rows, keys.shape[1])
    row_index = lax.broadcasted_iota(jnp.int32, shape, 0)
    visible = lax.broadcasted_iota(jnp.int32, shape, 1) <= positions_ref[0] + row_index
    visible = jnp.concatenate([visible] * per_head, axis=0)
    energy = jnp.zeros((1, 128), jnp.float32)
    for g in range(kv_heads):
        heads = [slice((g * per_head + i) * HEAD_DIM, (g * per_head + i + 1) * HEAD_DIM) for i in range(per_head)]
        grouped = jnp.concatenate([q[:, head] for head in heads], axis=0)
        here = slice(g * HEAD_DIM, (g + 1) * HEAD_DIM)
        copies[2 * g].wait()
        scores = lax.dot_general(
            grouped, k[:, here], (((1,), (1,)), ((), ())), preferred_element_type=jnp.float32
        ) * HEAD_DIM ** (-0.5)
        scores = jnp.where(visible, scores, -jnp.inf)
        weight = jnp.exp(scores - jnp.max(scores, axis=1, keepdims=True))
        probs = (weight / jnp.sum(weight, axis=1, keepdims=True)).astype(jnp.bfloat16)
        copies[2 * g + 1].wait()
        mix = jnp.dot(probs, v[:, here], preferred_element_type=jnp.float32).astype(jnp.bfloat16)
        for i, head in enumerate(heads):
            part = mix[i * rows : (i + 1) * rows]
            heads_ref[:, head] = part
            square = jnp.sum(jnp.square(part.astype(jnp.float32)), axis=0, keepdims=True)
            for lane in range(0, HEAD_DIM, 128):
                energy = energy + square[:, lane : lane + 128]
    energy_ref[...] = energy
    for copy in weights:
        copy.wait()


def attend(queries, cache_keys, cache_values, positions, enc, parts=8):
    rows, width = queries.shape
    slots, kv_width = cache_keys.shape[1:]
    kv_heads = kv_width // HEAD_DIM
    hbm = [pltpu.with_memory_space_constraint(x, pltpu.HBM) for x in (queries, cache_keys, cache_values, enc)]
    return kernel_call(
        functools.partial(attend_body, kv_heads, parts),
        [positions, *hbm],
        [IN_SMEM] + [IN_HBM] * 4,
        [half_array(rows, width), float_array(1, 128), pltpu.VMEM(enc.shape, enc.dtype)],
        [
            pltpu.VMEM((rows, width), jnp.bfloat16),
            pltpu.VMEM((slots, kv_width), jnp.bfloat16),
            pltpu.VMEM((slots, kv_width), jnp.bfloat16),
            pltpu.SemaphoreType.DMA((2 * kv_heads + 1,)),
            pltpu.SemaphoreType.DMA((parts,)),
        ],
        flops=4 * rows * slots * width,
    )


def load_body(parts, source, target, sems):
    size = source.shape[0] // parts
    copies = []
    for part in range(parts):
        here = pl.ds(part * size, size)
        copies.append(pltpu.make_async_copy(source.at[here], target.at[here], sems.at[part]))
    for copy in copies:
        copy.start()
    for copy in copies:
        copy.wait()


def load(x, parts=8):
    source = pltpu.with_memory_space_constraint(x, pltpu.HBM)
    return kernel_call(
        functools.partial(load_body, parts),
        [source],
        [IN_HBM],
        [pltpu.VMEM(x.shape, x.dtype)],
        [pltpu.SemaphoreType.DMA((parts,))],
    )[0]


def norms_body(block, dec_ref, column_ref, row_ref):
    for first in range(0, dec_ref.shape[0], block):
        here = slice(first, first + block)
        square = jnp.square(dec_ref[here, :].astype(jnp.float32))
        norms = jnp.sqrt(jnp.sum(square, axis=1, keepdims=True) + epsilon)
        column_ref[here, :] = norms
        row_ref[:, here] = jnp.broadcast_to(norms, (block, 128)).T[:1]


def decoder_norms(dec):
    latents = dec.shape[0]
    return kernel_call(
        functools.partial(norms_body, 256),
        [held(dec)],
        [IN_VMEM],
        [float_array(latents, 1), float_array(1, latents)],
    )


def codes(scaled):
    decay = jnp.exp2(-jnp.abs(scaled))
    small = decay * (LOG2E - (0.5 * LOG2E) * decay)
    soft = jnp.maximum(scaled, 0.0) + jnp.where(decay < 1e-3, small, jnp.log2(1.0 + decay))
    slope = jnp.exp2(scaled - soft)
    return soft * (1.0 / (sharpness * LOG2E)), slope.astype(jnp.bfloat16)


def norm_scale(energy_ref, entries):
    return lax.rsqrt(jnp.sum(energy_ref[...], axis=1, keepdims=True) / entries + epsilon)


def add_body(a_ref, b_ref, sum_ref):
    sum_ref[...] = a_ref[...] + b_ref[...]


def add(a, b):
    return kernel_call(add_body, [a, b], [IN_VMEM] * 2, [float_array(*a.shape)], limit=4)[0]


def join_body(halves, *refs):
    *pieces, out = refs
    if not halves:
        join(pieces, out)
        return
    cuts = [(first, piece.shape[0] // 2) for first in (0, 1) for piece in pieces]
    join(pieces * 2, out, [(first * size, size) for first, size in cuts])


def joined(*pieces, halves=False):
    count = sum(piece.shape[0] for piece in pieces)
    out = [half_array(count, pieces[0].shape[1])]
    body = functools.partial(join_body, halves)
    return kernel_call(body, pieces, [IN_VMEM] * len(pieces), out, limit=4)[0]


def add_split_body(a_ref, b_ref, keep_ref, send_ref):
    half = keep_ref.shape[0]
    keep_ref[...] = a_ref[:half] + b_ref[:half].astype(jnp.float32)
    send_ref[...] = (a_ref[half:] + b_ref[half:].astype(jnp.float32)).astype(jnp.bfloat16)


def add_split(a, b):
    half, width = a.shape[0] // 2, a.shape[1]
    outs = [float_array(half, width), half_array(half, width)]
    return kernel_call(add_split_body, [a, b], [IN_VMEM] * 2, outs, limit=4)


def add_both_body(a_ref, b_ref, sum_ref, send_ref):
    total = a_ref[...] + b_ref[...].astype(jnp.float32)
    sum_ref[...] = total
    send_ref[...] = total.astype(jnp.bfloat16)


def add_both(a, b):
    outs = [float_array(*a.shape), half_array(*a.shape)]
    return kernel_call(add_both_body, [a, b], [IN_VMEM] * 2, outs, limit=4)


def residual_body(entries, a_ref, b_ref, bias_ref, heads_ref, energy_ref, rebuilt_ref, residual_ref):
    half = rebuilt_ref.shape[0]
    scale = norm_scale(energy_ref, entries)
    for here, there in ((slice(0, half), slice(half, 2 * half)), (slice(half, 2 * half), slice(0, half))):
        rebuilt = a_ref[here] + b_ref[there].astype(jnp.float32) + bias_ref[...]
        inputs = (heads_ref[here].astype(jnp.float32) * scale).astype(jnp.bfloat16)
        residual_ref[here] = (rebuilt - inputs.astype(jnp.float32)).astype(jnp.bfloat16)
        if here.start == 0:
            rebuilt_ref[...] = rebuilt.astype(jnp.bfloat16)


def pair_residual(entries, *args):
    count, width = args[0].shape
    body = functools.partial(residual_body, entries)
    return kernel_call(body, args, [IN_VMEM] * 5, [half_array(count // 2, width), half_array(count, width)], limit=6)


def own_columns(x, own_ref, columns):
    return x[:, pl.ds(pl.multiple_of(own_ref[0] * columns, 128), columns)]


def join(pieces, rows, cuts=None):
    start = 0
    for piece, (first, size) in zip(pieces, cuts or [(0, piece.shape[0]) for piece in pieces], strict=True):
        rows[start : start + size] = piece[first : first + size]
        start += size


def whole(parts):
    return [(part, 0, part.shape[0]) for part in parts]


def encode_body(cuts, tile, entries, energy_ref, own_ref, enc_ref, bias_ref, *refs):
    count = len(cuts)
    pieces, (codes_ref, slope_ref, part_ref), (rows, *rest) = refs[:count], refs[count : count + 3], refs[count + 3 :]
    if rest:
        dec_ref, keep_ref, send_ref, rows, coded_ref = rows, *rest
    join(pieces, rows, cuts)
    factor = sharpness * LOG2E
    scale = norm_scale(energy_ref, entries) * factor
    for first in range(0, enc_ref.shape[1], tile):
        here = slice(first, first + tile)
        product = jnp.dot(rows[...], enc_ref[:, here], preferred_element_type=jnp.float32)
        coded, slope = codes(product * scale + bias_ref[:, here] * factor)
        codes_ref[here, :] = coded.T.astype(jnp.bfloat16)
        slope_ref[:, here] = slope
        if rest:
            coded_ref[:, here] = coded.astype(jnp.bfloat16)
    part = own_columns(rows, own_ref, part_ref.shape[0])
    part_ref[...] = part.astype(jnp.float32).T.astype(jnp.bfloat16)
    if rest:
        half = keep_ref.shape[0]
        for first in range(0, dec_ref.shape[1], tile):
            here = slice(first, first + tile)
            total = jnp.dot(coded_ref[...], dec_ref[:, here], preferred_element_type=jnp.float32)
            keep_ref[:, here] = total[:half]
            send_ref[:, here] = total[half:]


def cut_pieces(parts):
    return [part for part, _, _ in parts], [(first, size) for _, first, size in parts]


def encode(entries, energy, own, enc, bias, pieces, columns):
    width, latents = enc.shape
    pieces, cuts = cut_pieces(pieces)
    count = sum(size for _, size in cuts)
    return kernel_call(
        functools.partial(encode_body, cuts, min(512, latents), entries),
        [energy, own, held(enc), bias, *pieces],
        [IN_VMEM, IN_SMEM] + [IN_VMEM] * (2 + len(pieces)),
        [half_array(latents, count), half_array(count, latents), half_array(columns, count)],
        [pltpu.VMEM((count, width), jnp.bfloat16)],
        flops=2 * count * width * latents,
    )


def rebuild_body(cuts, tile, entries, energy_ref, own_ref, enc_ref, bias_ref, dec_ref, *refs):
    count = len(cuts)
    pieces, outs, scratch = refs[:count], refs[count : count + 5], refs[count + 5 :]
    encode_body(
        cuts, tile, entries, energy_ref, own_ref, enc_ref, bias_ref, *pieces, *outs[:3], dec_ref, *outs[3:], *scratch
    )


def encode_and_rebuild(entries, energy, own, enc, bias, dec, pieces, columns):
    width, latents = enc.shape
    pieces, cuts = cut_pieces(pieces)
    count = sum(size for _, size in cuts)
    return kernel_call(
        functools.partial(rebuild_body, cuts, min(512, latents), entries),
        [energy, own, held(enc), bias, held(dec), *pieces],
        [IN_VMEM, IN_SMEM] + [IN_VMEM] * (3 + len(pieces)),
        [
            half_array(latents, count),
            half_array(count, latents),
            half_array(columns, count),
            float_array(count // 2, width),
            float_array(count // 2, width),
        ],
        [pltpu.VMEM((count, width), jnp.bfloat16), pltpu.VMEM((count, latents), jnp.bfloat16)],
        flops=4 * count * width * latents,
    )


def pre_tile(rows, dec_ref, norms_ref, slope_ref, here, all_rows):
    product = lax.dot_general(
        rows[...], dec_ref[here, :], (((1,), (1,)), ((), ())), preferred_element_type=jnp.float32
    )
    grad = product * (2.0 / all_rows) + norms_ref[:, here] * (sparsity_weight / all_rows)
    return (grad * slope_ref[:, here].astype(jnp.float32)).astype(jnp.bfloat16)


def slope_body(cuts, tile, all_rows, own_ref, dec_ref, norms_ref, *refs):
    sets = len(cuts)
    slopes, refs = refs[:sets], refs[sets:]
    pieces = []
    for chosen in cuts:
        pieces.append(refs[: len(chosen)])
        refs = refs[len(chosen) :]
    grads, parts, scratch = refs[:sets], refs[sets : 2 * sets], refs[2 * sets :]
    for chosen, slope_ref, piece, grad_ref, part_ref, rows in zip(
        cuts, slopes, pieces, grads, parts, scratch, strict=True
    ):
        join(piece, rows, chosen)
        for first in range(0, dec_ref.shape[0], tile):
            here = slice(first, first + tile)
            grad_ref[:, here] = pre_tile(rows, dec_ref, norms_ref, slope_ref, here, all_rows)
        part_ref[...] = own_columns(rows, own_ref, part_ref.shape[1])


def pre_gradient(all_rows, own, dec, norms, slopes, sets, columns):
    latents, width = dec.shape
    cut_sets = [cut_pieces(pieces) for pieces in sets]
    counts = [sum(size for _, size in cuts) for _, cuts in cut_sets]
    args = [held(dec), norms, *slopes, *(part for parts, _ in cut_sets for part in parts)]
    outs = kernel_call(
        functools.partial(slope_body, [cuts for _, cuts in cut_sets], min(512, latents), all_rows),
        [own, *args],
        [IN_SMEM] + [IN_VMEM] * len(args),
        [half_array(count, latents) for count in counts] + [half_array(count, columns) for count in counts],
        [pltpu.VMEM((count, width), jnp.bfloat16) for count in counts],
        flops=2 * sum(counts) * width * latents,
    )
    return list(zip(outs[: len(sets)], outs[len(sets) :], strict=True))


def early_body(groups, tile, *refs):
    rows, grads, coded, residual = (refs[i * groups : (i + 1) * groups] for i in range(4))
    enc_ref, dec_ref, sums_ref = refs[4 * groups :]
    for first in range(0, enc_ref.shape[1], tile):
        here = slice(first, first + tile)
        enc, dec, sums = 0.0, 0.0, 0.0
        for g in range(groups):
            enc = enc + jnp.dot(rows[g][...], grads[g][:, here], preferred_element_type=jnp.float32)
            dec = dec + jnp.dot(coded[g][here, :], residual[g][...], preferred_element_type=jnp.float32)
            sums = sums + jnp.sum(coded[g][here, :].astype(jnp.float32), axis=1, keepdims=True)
        enc_ref[:, here] = enc
        dec_ref[here, :] = dec
        sums_ref[here, :] = sums


def early_sums(rows, grads, coded, residual):
    columns = rows[0].shape[0]
    latents = coded[0].shape[0]
    count = sum(x.shape[0] for x in grads)
    args = [*rows, *grads, *coded, *residual]
    return kernel_call(
        functools.partial(early_body, len(rows), min(512, latents)),
        args,
        [IN_VMEM] * len(args),
        [float_array(columns, latents), float_array(latents, columns), float_array(latents, 1)],
        flops=4 * count * columns * latents,
    )


def last_body(
    cuts, groups, tile, all_rows, entries, energy_ref, own_ref, column_ref, row_ref, dec_ref, enc_sum, dec_sum,
    sums_ref, rows_ref, coded_ref, slope_ref, *refs,
):
    rows, grads, coded, parts = (refs[i * groups : (i + 1) * groups] for i in range(4))
    refs = refs[4 * groups :]
    count = len(cuts)
    pieces, (enc_out, dec_out, enc_buffer, dec_buffer, residual, part, sems) = refs[:count], refs[count:]
    columns = dec_buffer.shape[2]
    steps = dec_ref.shape[0] // tile
    scale = norm_scale(energy_ref, entries)
    join(pieces, residual, cuts)
    part[...] = own_columns(residual, own_ref, columns)

    def copies(step):
        slot, here = step % 2, pl.ds(step * tile, tile)
        return (
            pltpu.make_async_copy(enc_buffer.at[slot], enc_out.at[:, here], sems.at[slot, 0]),
            pltpu.make_async_copy(dec_buffer.at[slot], dec_out.at[here], sems.at[slot, 1]),
        )

    for step in range(steps):
        if step >= 2:
            for copy in copies(step - 2):
                copy.wait()
        here = slice(step * tile, (step + 1) * tile)
        enc, dec, sums = enc_sum[:, here], dec_sum[here, :], sums_ref[here, :]
        for coded_set, part_set in zip((*coded, coded_ref), (*parts, part), strict=True):
            dec = dec + jnp.dot(coded_set[here, :], part_set[...], preferred_element_type=jnp.float32)
            sums = sums + jnp.sum(coded_set[here, :].astype(jnp.float32), axis=1, keepdims=True)
        weights = own_columns(dec_ref.at[here, :], own_ref, columns).astype(jnp.float32)
        factor = sums / column_ref[here, :] * (sparsity_weight / all_rows)
        dec_buffer[step % 2] = dec * (2.0 / all_rows) + factor * weights
        copies(step)[1].start()
        for rows_set, grad in zip(rows, grads, strict=True):
            enc = enc + jnp.dot(rows_set[...], grad[:, here], preferred_element_type=jnp.float32)
        grad = pre_tile(residual, dec_ref, row_ref, slope_ref, here, all_rows)
        enc = enc + jnp.dot(rows_ref[...], grad, preferred_element_type=jnp.float32)
        enc_buffer[step % 2] = enc * scale
        copies(step)[0].start()
    for step in range(max(steps - 2, 0), steps):
        for copy in copies(step):
            copy.wait()


def weight_gradients(all_rows, entries, energy, own, column, row, dec, early, middle, encoded, pieces):
    coded, slope, rows = encoded
    columns = rows.shape[0]
    latents, width = dec.shape
    pieces, cuts = cut_pieces(pieces)
    count = sum(size for _, size in cuts)
    tile = min(512, latents)
    middle = [x for kind in zip(*middle, strict=True) for x in kind]
    args = [column, row, held(dec), *early, rows, coded, slope, *middle, *pieces]
    return kernel_call(
        functools.partial(last_body, cuts, len(middle) // 4, tile, all_rows, entries),
        [energy, own, *args],
        [IN_VMEM, IN_SMEM] + [IN_VMEM] * len(args),
        [pltpu.HBM((columns, latents), jnp.float32), pltpu.HBM((latents, columns), jnp.float32)],
        [
            pltpu.VMEM((2, columns, tile), jnp.float32),
            pltpu.VMEM((2, tile, columns), jnp.float32),
            pltpu.VMEM((count, width), jnp.bfloat16),
            pltpu.VMEM((count, columns), jnp.bfloat16),
            pltpu.SemaphoreType.DMA((2, 2)),
        ],
        [IN_HBM, IN_HBM],
        flops=2 * count * width * latents + 4 * count * columns * latents,
        limit=16,
    )


def bits(size):
    found, bit = [], 1
    while bit < size:
        found.append(bit)
        bit *= 2
    return found


def swap(x, even, odd=None):
    count = lax.axis_size("dp") * lax.axis_size("latent")
    odd = even if odd is None else odd
    return lax.ppermute(
        x, ("dp", "latent"), [(i, i ^ (odd if i & 1 else even)) for i in range(count)]
    )


def line_steps():
    steps = bits(lax.axis_size("latent"))[1:]
    return list(zip(steps[::-1], steps, strict=True))


def plane_steps():
    latent_size = lax.axis_size("latent")
    steps = [bit * latent_size for bit in bits(lax.axis_size("dp"))]
    return list(zip(steps, steps[::-1], strict=True))


def after(value, *done):
    return lax.optimization_barrier((value, *done))[0]


def after(value, *done):
    return lax.optimization_barrier((value, *done))[0]


def send_body(group_bits, own_ref, shuffle_ref, rows_ref, *outs):
    count, width = rows_ref.shape
    per_peer = outs[0].shape[0]
    goes_to = lax.shift_right_logical(shuffle_ref[...], group_bits) ^ own_ref[0]
    slot = shuffle_ref[...] & (count - 1)
    over_lanes = (((1,), (1,)), ((), ()))
    sublane = lax.broadcasted_iota(jnp.int32, (count, count), 0)
    lane = lax.broadcasted_iota(jnp.int32, (count, count), 1)
    peer_row = jnp.broadcast_to(goes_to, (count, count)).astype(jnp.float32)
    one_hot = (sublane == lane).astype(jnp.bfloat16)
    peer_column = lax.dot_general(
        one_hot, peer_row.astype(jnp.bfloat16), over_lanes, preferred_element_type=jnp.float32
    )
    before = (peer_column == peer_row) & (sublane < lane)
    rank = jnp.sum(before.astype(jnp.float32), axis=0, keepdims=True)
    order = goes_to.astype(jnp.float32) * per_peer + rank
    pick = (order == sublane.astype(jnp.float32)).astype(jnp.bfloat16)
    rows = jnp.dot(pick, rows_ref[...], preferred_element_type=jnp.float32)
    slot_rows = jnp.broadcast_to(slot, (128, count)).astype(jnp.float32).astype(jnp.bfloat16)
    slots = lax.dot_general(pick, slot_rows, over_lanes, preferred_element_type=jnp.float32)
    for peer, out in enumerate(outs):
        here = slice(peer * per_peer, (peer + 1) * per_peer)
        out[:, :width] = rows[here]
        out[:, width:] = slots[here]


def place_body(*refs):
    *pieces, out_ref, rows = refs
    join(pieces, rows)
    width = out_ref.shape[1]
    index = lax.broadcasted_iota(jnp.int32, (rows.shape[0], rows.shape[0]), 1).astype(jnp.float32)
    pick = (rows[:, width : width + 1] == index).astype(jnp.bfloat16)
    out_ref[...] = lax.dot_general(
        pick, rows[:, :width].astype(jnp.bfloat16), (((0,), (0,)), ((), ())), preferred_element_type=jnp.float32
    ).astype(jnp.bfloat16)


def send_rows(own, rows, shuffle):
    data_size = lax.axis_size("dp")
    latent_size = lax.axis_size("latent")
    count, width = rows.shape
    out = float_array(count // data_size, width + 128)
    body = functools.partial(send_body, len(bits(count * latent_size)))
    specs = [IN_SMEM, IN_VMEM, IN_VMEM]
    sent = kernel_call(body, [own, shuffle, rows], specs, [out] * data_size, limit=4)
    return [swap(x, peer * latent_size) if peer else x for peer, x in enumerate(sent)]


def place_rows(arrived, count, width):
    scratch = [pltpu.VMEM((count, width + 128), jnp.float32)]
    specs = [IN_VMEM] * len(arrived)
    return kernel_call(place_body, arrived, specs, [half_array(count, width)], scratch, limit=4)[0]


def shards(
    queries,
    cache_keys,
    cache_values,
    positions,
    shuffle,
    enc_weight,
    enc_bias,
    dec_weight,
    dec_bias,
):
    rows_here = queries.shape[0]
    att_width = queries.shape[1]
    data_size = lax.axis_size("dp")
    latent_size = lax.axis_size("latent")
    all_rows = rows_here * data_size * latent_size
    columns = att_width // data_size
    entries = all_rows * att_width
    core = (1, 1)
    line, plane = line_steps(), plane_steps()
    own = lax.axis_index("dp").astype(jnp.int32).reshape(1)
    bias, out_bias, places, own = lax.optimization_barrier(
        (enc_bias[None, :], dec_bias[None, :], shuffle[None, :], own)
    )
    heads_out, energy, enc = attend(queries, cache_keys, cache_values, positions, after(enc_weight, bias, out_bias, places, own))

    small_steps = plane + [core] + line
    rows = heads_out
    for number, mask in enumerate(line):
        arrived = swap(rows, *mask)
        count = len(plane) if number == 0 else 1
        if number == len(line) - 1:
            count = len(small_steps)
        for small in small_steps[:count]:
            other = swap(energy, *small)
            if small == line[0]:
                dec = load(after(dec_weight, energy))
                other = after(other, dec)
            energy = add(energy, other)
        small_steps = small_steps[count:]
        rows = joined(rows, after(arrived, energy))
        if number == 0:
            pair = rows

    def chunks(near, far, first, size, largest=256):
        step = min(size, largest)
        return [[(near, i, step), (far, i, step)] for i in range(first, first + size, step)]

    hop = swap(rows, *plane[0])
    group = whole([rows, swap(rows, *core)])
    *first_set, keep, send = encode_and_rebuild(entries, energy, own, enc, bias, dec, group, columns)
    encoded = [first_set]

    def encode_next(parts, now):
        parts = [(after(part, now), *cut) for part, *cut in parts]
        encoded.append(encode(entries, energy, own, enc, bias, parts, columns))
        return encoded[-1][0]

    arrived = swap(after(send, hop), *core)
    total = keep
    far = [rows, hop]
    for number, mask in enumerate(line[::-1]):
        last = number == len(line) - 1
        total, sent = (add_both if last else add_split)(total, arrived)
        arrived = swap(sent, *mask)
        if number == 0:
            hop = after(hop, sent)
            arrived = after(arrived, encode_next(whole([hop, swap(hop, *core)]), sent))
            for step in plane[1:2]:
                far.append(swap(joined(*(after(piece, sent) for piece in far), halves=True), *step))
        if last:
            norms_column, norms_row = decoder_norms(after(dec, sent))
            arrived = after(arrived, norms_row, far[-1])
    rebuilt_own, rows = pair_residual(entries, total, arrived, out_bias, pair, energy)
    for step in plane[2:]:
        far.append(swap(joined(*(after(piece, rows) for piece in far), halves=True), *step))
    others = [swap(after(piece, rows), *core) for piece in far[2:]]

    for mask in line[1:-1]:
        rows = joined(rows, swap(rows, *mask))
    near, late = [rows], [swap(rows, *line[-1])]
    near.append(swap(rows, *plane[0]))
    done = []
    for piece, other in zip(far[2:], others, strict=True):
        half = piece.shape[0] // 2
        for first in (0, half):
            done += [encode_next(parts, rows) for parts in chunks(piece, other, first, half)]
    late[0] = after(late[0], near[1], *done)
    grads = []

    def pre(sets, now):
        slopes = [code[1] for code in encoded[len(grads) : len(grads) + len(sets)]]
        sets = [[(after(part, now), *cut) for part, *cut in parts] for parts in sets]
        grads.extend(pre_gradient(all_rows, own, dec, norms_row, slopes, sets, columns))
        return grads[-1][0]

    def ready(sets):
        chosen = [(encoded[i], grads[i]) for i in sets]
        return [(code[2], grad[0], code[0], grad[1]) for code, grad in chosen]

    late.append(swap(late[0], *plane[0]))
    near.append(swap(joined(*near), *plane[1]))
    rows = joined(near[0], late[0])
    done = pre([whole([rows, swap(rows, *core)])], rows)
    moved = send_rows(own, after(rebuilt_own, rows), places)
    near[2] = after(near[2], done)
    hop = joined(near[1], after(late[1], done))
    sets = [whole([hop, swap(hop, *core)])]
    count = 2
    for number, step in enumerate(plane[1:], 1):
        if number > 1:
            near.append(swap(joined(*near), *step))
        late.append(swap(joined(*late), *step))
        sets += chunks(near[-1], swap(near[-1], *core), 0, near[-1].shape[0])
        if number < len(plane) - 1:
            sets += chunks(late[-1], swap(late[-1], *core), 0, late[-1].shape[0])
            count += 2 * len(chunks(near[-1], near[-1], 0, near[-1].shape[0]))
    for first in range(0, len(sets), 2):
        done = pre(sets[first : first + 2], hop)
    last = after(late[-1], done, *moved)
    sets = chunks(last, swap(last, *core), 0, last.shape[0])
    for parts in sets[:-1]:
        done = pre([parts], done)
    early = early_sums(*([after(x, last) for x in kind] for kind in zip(*ready(range(count)), strict=True)))
    grad_enc, grad_dec = weight_gradients(
        all_rows,
        entries,
        energy,
        own,
        norms_column,
        norms_row,
        dec,
        early,
        ready(range(count, len(grads))),
        encoded[-1],
        sets[-1],
    )
    rebuilt = place_rows([after(part, early[0]) for part in moved], rows_here, att_width)
    return (rebuilt, grad_enc, grad_dec)


def solution(mesh):
    in_specs = (
        P(("dp", "latent"), None),
        P(("dp", "latent"), None, None),
        P(("dp", "latent"), None, None),
        P(("dp", "latent")),
        P(("dp", "latent")),
        P(None, "latent"),
        P("latent"),
        P("latent", None),
        P(),
    )
    out_specs = (P(("dp", "latent"), None), P("dp", "latent"), P("latent", "dp"))
    return jax.shard_map(shards, mesh=mesh, in_specs=in_specs, out_specs=out_specs, check_vma=False)
```

```python
import functools

import jax
import jax.numpy as jnp
from jax import lax
from jax.experimental import pallas as pl
from jax.experimental.pallas import tpu as pltpu
from jax.sharding import PartitionSpec as P

HEAD_DIM = 256


sharpness = 4.0
sparsity_weight = 1.0
epsilon = 1e-06

MIB = 1024 * 1024
LOG2E = 1.4426950408889634
IN_VMEM = pl.BlockSpec(memory_space=pltpu.VMEM)
IN_HBM = pl.BlockSpec(memory_space=pltpu.HBM)
IN_SMEM = pl.BlockSpec(memory_space=pltpu.SMEM)


def kernel_call(body, args, specs, outs, scratch=(), out_specs=None, flops=0, limit=12):
    return pl.pallas_call(
        body,
        in_specs=specs,
        out_specs=out_specs or [IN_VMEM] * len(outs),
        out_shape=outs,
        scratch_shapes=list(scratch),
        compiler_params=pltpu.CompilerParams(vmem_limit_bytes=limit * MIB),
        cost_estimate=pl.CostEstimate(flops=flops, bytes_accessed=0, transcendentals=0),
    )(*args)


def held(x):
    return pltpu.with_memory_space_constraint(x, pltpu.VMEM)


def half_array(*shape):
    return jax.ShapeDtypeStruct(shape, jnp.bfloat16)


def float_array(*shape):
    return jax.ShapeDtypeStruct(shape, jnp.float32)


def attend_body(
    kv_heads, parts, positions_ref, queries, keys, values, enc, heads_ref, energy_ref, enc_ref, q, k, v, sems, enc_sems
):
    rows, width = q.shape
    per_head = width // kv_heads // HEAD_DIM
    whole = pltpu.make_async_copy(queries, q, sems.at[2 * kv_heads])
    whole.start()
    copies = []
    for g in range(kv_heads):
        here = pl.ds(g * HEAD_DIM, HEAD_DIM)
        copies.append(pltpu.make_async_copy(keys.at[0, :, here], k.at[:, here], sems.at[2 * g]))
        copies.append(pltpu.make_async_copy(values.at[0, :, here], v.at[:, here], sems.at[2 * g + 1]))
    size = enc.shape[0] // parts
    weights = []
    for part in range(parts):
        here = pl.ds(part * size, size)
        weights.append(pltpu.make_async_copy(enc.at[here], enc_ref.at[here], enc_sems.at[part]))
    for copy in copies + weights:
        copy.start()
    whole.wait()
    shape = (rows, keys.shape[1])
    row_index = lax.broadcasted_iota(jnp.int32, shape, 0)
    visible = lax.broadcasted_iota(jnp.int32, shape, 1) <= positions_ref[0] + row_index
    visible = jnp.concatenate([visible] * per_head, axis=0)
    energy = jnp.zeros((1, 128), jnp.float32)
    for g in range(kv_heads):
        heads = [slice((g * per_head + i) * HEAD_DIM, (g * per_head + i + 1) * HEAD_DIM) for i in range(per_head)]
        grouped = jnp.concatenate([q[:, head] for head in heads], axis=0)
        here = slice(g * HEAD_DIM, (g + 1) * HEAD_DIM)
        copies[2 * g].wait()
        scores = lax.dot_general(
            grouped, k[:, here], (((1,), (1,)), ((), ())), preferred_element_type=jnp.float32
        ) * HEAD_DIM ** (-0.5)
        scores = jnp.where(visible, scores, -jnp.inf)
        weight = jnp.exp(scores - jnp.max(scores, axis=1, keepdims=True))
        probs = (weight / jnp.sum(weight, axis=1, keepdims=True)).astype(jnp.bfloat16)
        copies[2 * g + 1].wait()
        mix = jnp.dot(probs, v[:, here], preferred_element_type=jnp.float32).astype(jnp.bfloat16)
        for i, head in enumerate(heads):
            part = mix[i * rows : (i + 1) * rows]
            heads_ref[:, head] = part
            square = jnp.sum(jnp.square(part.astype(jnp.float32)), axis=0, keepdims=True)
            for lane in range(0, HEAD_DIM, 128):
                energy = energy + square[:, lane : lane + 128]
    energy_ref[...] = energy
    for copy in weights:
        copy.wait()


def attend(queries, cache_keys, cache_values, positions, enc, parts=8):
    rows, width = queries.shape
    slots, kv_width = cache_keys.shape[1:]
    kv_heads = kv_width // HEAD_DIM
    hbm = [pltpu.with_memory_space_constraint(x, pltpu.HBM) for x in (queries, cache_keys, cache_values, enc)]
    return kernel_call(
        functools.partial(attend_body, kv_heads, parts),
        [positions, *hbm],
        [IN_SMEM] + [IN_HBM] * 4,
        [half_array(rows, width), float_array(1, 128), pltpu.VMEM(enc.shape, enc.dtype)],
        [
            pltpu.VMEM((rows, width), jnp.bfloat16),
            pltpu.VMEM((slots, kv_width), jnp.bfloat16),
            pltpu.VMEM((slots, kv_width), jnp.bfloat16),
            pltpu.SemaphoreType.DMA((2 * kv_heads + 1,)),
            pltpu.SemaphoreType.DMA((parts,)),
        ],
        flops=4 * rows * slots * width,
    )


def load_body(parts, source, target, sems):
    size = source.shape[0] // parts
    copies = []
    for part in range(parts):
        here = pl.ds(part * size, size)
        copies.append(pltpu.make_async_copy(source.at[here], target.at[here], sems.at[part]))
    for copy in copies:
        copy.start()
    for copy in copies:
        copy.wait()


def load(x, parts=8):
    source = pltpu.with_memory_space_constraint(x, pltpu.HBM)
    return kernel_call(
        functools.partial(load_body, parts),
        [source],
        [IN_HBM],
        [pltpu.VMEM(x.shape, x.dtype)],
        [pltpu.SemaphoreType.DMA((parts,))],
    )[0]


def norms_body(block, dec_ref, column_ref, row_ref):
    for first in range(0, dec_ref.shape[0], block):
        here = slice(first, first + block)
        square = jnp.square(dec_ref[here, :].astype(jnp.float32))
        norms = jnp.sqrt(jnp.sum(square, axis=1, keepdims=True) + epsilon)
        column_ref[here, :] = norms
        row_ref[:, here] = jnp.broadcast_to(norms, (block, 128)).T[:1]


def decoder_norms(dec):
    latents = dec.shape[0]
    return kernel_call(
        functools.partial(norms_body, 256),
        [held(dec)],
        [IN_VMEM],
        [float_array(latents, 1), float_array(1, latents)],
    )


def codes(scaled):
    decay = jnp.exp2(-jnp.abs(scaled))
    small = decay * (LOG2E - (0.5 * LOG2E) * decay)
    soft = jnp.maximum(scaled, 0.0) + jnp.where(decay < 1e-3, small, jnp.log2(1.0 + decay))
    slope = jnp.exp2(scaled - soft)
    return soft * (1.0 / (sharpness * LOG2E)), slope.astype(jnp.bfloat16)


def norm_scale(energy_ref, entries):
    return lax.rsqrt(jnp.sum(energy_ref[...], axis=1, keepdims=True) / entries + epsilon)


def add_body(a_ref, b_ref, sum_ref):
    sum_ref[...] = a_ref[...] + b_ref[...]


def add(a, b):
    return kernel_call(add_body, [a, b], [IN_VMEM] * 2, [float_array(*a.shape)], limit=4)[0]


def join_body(halves, *refs):
    *pieces, out = refs
    if not halves:
        join(pieces, out)
        return
    cuts = [(first, piece.shape[0] // 2) for first in (0, 1) for piece in pieces]
    join(pieces * 2, out, [(first * size, size) for first, size in cuts])


def joined(*pieces, halves=False):
    count = sum(piece.shape[0] for piece in pieces)
    out = [half_array(count, pieces[0].shape[1])]
    body = functools.partial(join_body, halves)
    limit = 4 + max(0, count - 256) // 64
    return kernel_call(body, pieces, [IN_VMEM] * len(pieces), out, limit=limit)[0]


def add_split_body(a_ref, b_ref, keep_ref, send_ref):
    half = keep_ref.shape[0]
    keep_ref[...] = a_ref[:half] + b_ref[:half].astype(jnp.float32)
    send_ref[...] = (a_ref[half:] + b_ref[half:].astype(jnp.float32)).astype(jnp.bfloat16)


def add_split(a, b):
    half, width = a.shape[0] // 2, a.shape[1]
    outs = [float_array(half, width), half_array(half, width)]
    return kernel_call(add_split_body, [a, b], [IN_VMEM] * 2, outs, limit=4)


def add_both_body(a_ref, b_ref, sum_ref, send_ref):
    total = a_ref[...] + b_ref[...].astype(jnp.float32)
    sum_ref[...] = total
    send_ref[...] = total.astype(jnp.bfloat16)


def add_both(a, b):
    outs = [float_array(*a.shape), half_array(*a.shape)]
    return kernel_call(add_both_body, [a, b], [IN_VMEM] * 2, outs, limit=4)


def residual_body(entries, a_ref, b_ref, bias_ref, heads_ref, energy_ref, rebuilt_ref, residual_ref):
    half = rebuilt_ref.shape[0]
    scale = norm_scale(energy_ref, entries)
    for here, there in ((slice(0, half), slice(half, 2 * half)), (slice(half, 2 * half), slice(0, half))):
        rebuilt = a_ref[here] + b_ref[there].astype(jnp.float32) + bias_ref[...]
        inputs = (heads_ref[here].astype(jnp.float32) * scale).astype(jnp.bfloat16)
        residual_ref[here] = (rebuilt - inputs.astype(jnp.float32)).astype(jnp.bfloat16)
        if here.start == 0:
            rebuilt_ref[...] = rebuilt.astype(jnp.bfloat16)


def pair_residual(entries, *args):
    count, width = args[0].shape
    body = functools.partial(residual_body, entries)
    return kernel_call(body, args, [IN_VMEM] * 5, [half_array(count // 2, width), half_array(count, width)], limit=6)


def own_columns(x, own_ref, columns):
    return x[:, pl.ds(pl.multiple_of(own_ref[0] * columns, 128), columns)]


def join(pieces, rows, cuts=None):
    start = 0
    for piece, (first, size) in zip(pieces, cuts or [(0, piece.shape[0]) for piece in pieces], strict=True):
        rows[start : start + size] = piece[first : first + size]
        start += size


def whole(parts):
    return [(part, 0, part.shape[0]) for part in parts]


def encode_body(cuts, tile, entries, energy_ref, own_ref, enc_ref, bias_ref, *refs):
    count = len(cuts)
    pieces, (codes_ref, slope_ref, part_ref), (rows, *rest) = refs[:count], refs[count : count + 3], refs[count + 3 :]
    if rest:
        dec_ref, keep_ref, send_ref, rows, coded_ref = rows, *rest
    join(pieces, rows, cuts)
    factor = sharpness * LOG2E
    scale = norm_scale(energy_ref, entries) * factor
    for first in range(0, enc_ref.shape[1], tile):
        here = slice(first, first + tile)
        product = jnp.dot(rows[...], enc_ref[:, here], preferred_element_type=jnp.float32)
        coded, slope = codes(product * scale + bias_ref[:, here] * factor)
        codes_ref[here, :] = coded.T.astype(jnp.bfloat16)
        slope_ref[:, here] = slope
        if rest:
            coded_ref[:, here] = coded.astype(jnp.bfloat16)
    part = own_columns(rows, own_ref, part_ref.shape[0])
    part_ref[...] = part.astype(jnp.float32).T.astype(jnp.bfloat16)
    if rest:
        half = keep_ref.shape[0]
        for first in range(0, dec_ref.shape[1], tile):
            here = slice(first, first + tile)
            total = jnp.dot(coded_ref[...], dec_ref[:, here], preferred_element_type=jnp.float32)
            keep_ref[:, here] = total[:half]
            send_ref[:, here] = total[half:]


def cut_pieces(parts):
    return [part for part, _, _ in parts], [(first, size) for _, first, size in parts]


def encode(entries, energy, own, enc, bias, pieces, columns):
    width, latents = enc.shape
    pieces, cuts = cut_pieces(pieces)
    count = sum(size for _, size in cuts)
    return kernel_call(
        functools.partial(encode_body, cuts, min(512, latents), entries),
        [energy, own, held(enc), bias, *pieces],
        [IN_VMEM, IN_SMEM] + [IN_VMEM] * (2 + len(pieces)),
        [half_array(latents, count), half_array(count, latents), half_array(columns, count)],
        [pltpu.VMEM((count, width), jnp.bfloat16)],
        flops=2 * count * width * latents,
    )


def rebuild_body(cuts, tile, entries, energy_ref, own_ref, enc_ref, bias_ref, dec_ref, *refs):
    count = len(cuts)
    pieces, outs, scratch = refs[:count], refs[count : count + 5], refs[count + 5 :]
    encode_body(
        cuts, tile, entries, energy_ref, own_ref, enc_ref, bias_ref, *pieces, *outs[:3], dec_ref, *outs[3:], *scratch
    )


def encode_and_rebuild(entries, energy, own, enc, bias, dec, pieces, columns):
    width, latents = enc.shape
    pieces, cuts = cut_pieces(pieces)
    count = sum(size for _, size in cuts)
    return kernel_call(
        functools.partial(rebuild_body, cuts, min(512, latents), entries),
        [energy, own, held(enc), bias, held(dec), *pieces],
        [IN_VMEM, IN_SMEM] + [IN_VMEM] * (3 + len(pieces)),
        [
            half_array(latents, count),
            half_array(count, latents),
            half_array(columns, count),
            float_array(count // 2, width),
            float_array(count // 2, width),
        ],
        [pltpu.VMEM((count, width), jnp.bfloat16), pltpu.VMEM((count, latents), jnp.bfloat16)],
        flops=4 * count * width * latents,
    )


def pre_tile(rows, dec_ref, norms_ref, slope_ref, here, all_rows):
    product = lax.dot_general(
        rows[...], dec_ref[here, :], (((1,), (1,)), ((), ())), preferred_element_type=jnp.float32
    )
    grad = product * (2.0 / all_rows) + norms_ref[:, here] * (sparsity_weight / all_rows)
    return (grad * slope_ref[:, here].astype(jnp.float32)).astype(jnp.bfloat16)


def slope_body(cuts, tile, all_rows, own_ref, dec_ref, norms_ref, *refs):
    sets = len(cuts)
    slopes, refs = refs[:sets], refs[sets:]
    pieces = []
    for chosen in cuts:
        pieces.append(refs[: len(chosen)])
        refs = refs[len(chosen) :]
    grads, parts, scratch = refs[:sets], refs[sets : 2 * sets], refs[2 * sets :]
    for chosen, slope_ref, piece, grad_ref, part_ref, rows in zip(
        cuts, slopes, pieces, grads, parts, scratch, strict=True
    ):
        join(piece, rows, chosen)
        for first in range(0, dec_ref.shape[0], tile):
            here = slice(first, first + tile)
            grad_ref[:, here] = pre_tile(rows, dec_ref, norms_ref, slope_ref, here, all_rows)
        part_ref[...] = own_columns(rows, own_ref, part_ref.shape[1])


def pre_gradient(all_rows, own, dec, norms, slopes, sets, columns):
    latents, width = dec.shape
    cut_sets = [cut_pieces(pieces) for pieces in sets]
    counts = [sum(size for _, size in cuts) for _, cuts in cut_sets]
    args = [held(dec), norms, *slopes, *(part for parts, _ in cut_sets for part in parts)]
    outs = kernel_call(
        functools.partial(slope_body, [cuts for _, cuts in cut_sets], min(512, latents), all_rows),
        [own, *args],
        [IN_SMEM] + [IN_VMEM] * len(args),
        [half_array(count, latents) for count in counts] + [half_array(count, columns) for count in counts],
        [pltpu.VMEM((count, width), jnp.bfloat16) for count in counts],
        flops=2 * sum(counts) * width * latents,
        limit=12 + max(0, sum(counts) - 512) // 32,
    )
    return list(zip(outs[: len(sets)], outs[len(sets) :], strict=True))


def early_body(cuts, given, tile, all_rows, own_ref, dec_ref, norms_ref, *refs):
    sets = len(cuts)
    rows, coded, slopes, refs = refs[: sets + given], refs[sets + given : 2 * (sets + given)], refs[2 * (sets + given) :][:sets], refs[2 * (sets + given) + sets :]
    grads, parts, refs = refs[:given], refs[given : 2 * given], refs[2 * given :]
    pieces = []
    for chosen in cuts:
        pieces.append(refs[: len(chosen)])
        refs = refs[len(chosen) :]
    (enc_ref, dec_sum, sums_ref), scratch = refs[:3], refs[3:]
    residuals, own_parts = scratch[:sets], scratch[sets:]
    for chosen, piece, residual, part in zip(cuts, pieces, residuals, own_parts, strict=True):
        join(piece, residual, chosen)
        part[...] = own_columns(residual, own_ref, part.shape[1])
    for first in range(0, dec_ref.shape[0], tile):
        here = slice(first, first + tile)
        made = [
            pre_tile(residual, dec_ref, norms_ref, slope_ref, here, all_rows)
            for residual, slope_ref in zip(residuals, slopes, strict=True)
        ]
        enc, dec, sums = 0.0, 0.0, 0.0
        for rows_set, grad in zip(rows, [grad[:, here] for grad in grads] + made, strict=True):
            enc = enc + jnp.dot(rows_set[...], grad, preferred_element_type=jnp.float32)
        for coded_set, part in zip(coded, (*parts, *own_parts), strict=True):
            dec = dec + jnp.dot(coded_set[here, :], part[...], preferred_element_type=jnp.float32)
            sums = sums + jnp.sum(coded_set[here, :].astype(jnp.float32), axis=1, keepdims=True)
        enc_ref[:, here] = enc
        dec_sum[here, :] = dec
        sums_ref[here, :] = sums


def early_sums(all_rows, own, dec, norms, encoded, grads, sets):
    latents, width = dec.shape
    columns = encoded[0][2].shape[0]
    cut_sets = [cut_pieces(pieces) for pieces in sets]
    counts = [sum(size for _, size in cuts) for _, cuts in cut_sets]
    args = [held(dec), norms, *(x[2] for x in encoded), *(x[0] for x in encoded)]
    args += [x[1] for x in encoded[len(grads) :]] + [x[0] for x in grads] + [x[1] for x in grads]
    args += [part for parts, _ in cut_sets for part in parts]
    return kernel_call(
        functools.partial(early_body, [cuts for _, cuts in cut_sets], len(grads), min(512, latents), all_rows),
        [own, *args],
        [IN_SMEM] + [IN_VMEM] * len(args),
        [float_array(columns, latents), float_array(latents, columns), float_array(latents, 1)],
        [pltpu.VMEM((count, width), jnp.bfloat16) for count in counts]
        + [pltpu.VMEM((count, columns), jnp.bfloat16) for count in counts],
        flops=2 * sum(counts) * width * latents,
        limit=16 + max(0, sum(counts) - 512) // 32,
    )


def last_body(
    cuts, groups, tile, all_rows, entries, energy_ref, own_ref, column_ref, row_ref, dec_ref, enc_sum, dec_sum,
    sums_ref, rows_ref, coded_ref, slope_ref, *refs,
):
    rows, grads, coded, parts = (refs[i * groups : (i + 1) * groups] for i in range(4))
    refs = refs[4 * groups :]
    count = len(cuts)
    pieces, (enc_out, dec_out, enc_buffer, dec_buffer, residual, part, sems) = refs[:count], refs[count:]
    columns = dec_buffer.shape[2]
    steps = dec_ref.shape[0] // tile
    scale = norm_scale(energy_ref, entries)
    join(pieces, residual, cuts)
    part[...] = own_columns(residual, own_ref, columns)

    def copies(step):
        slot, here = step % 2, pl.ds(step * tile, tile)
        return (
            pltpu.make_async_copy(enc_buffer.at[slot], enc_out.at[:, here], sems.at[slot, 0]),
            pltpu.make_async_copy(dec_buffer.at[slot], dec_out.at[here], sems.at[slot, 1]),
        )

    for step in range(steps):
        if step >= 2:
            for copy in copies(step - 2):
                copy.wait()
        here = slice(step * tile, (step + 1) * tile)
        enc, dec, sums = enc_sum[:, here], dec_sum[here, :], sums_ref[here, :]
        for coded_set, part_set in zip((*coded, coded_ref), (*parts, part), strict=True):
            dec = dec + jnp.dot(coded_set[here, :], part_set[...], preferred_element_type=jnp.float32)
            sums = sums + jnp.sum(coded_set[here, :].astype(jnp.float32), axis=1, keepdims=True)
        weights = own_columns(dec_ref.at[here, :], own_ref, columns).astype(jnp.float32)
        factor = sums / column_ref[here, :] * (sparsity_weight / all_rows)
        dec_buffer[step % 2] = dec * (2.0 / all_rows) + factor * weights
        copies(step)[1].start()
        for rows_set, grad in zip(rows, grads, strict=True):
            enc = enc + jnp.dot(rows_set[...], grad[:, here], preferred_element_type=jnp.float32)
        grad = pre_tile(residual, dec_ref, row_ref, slope_ref, here, all_rows)
        enc = enc + jnp.dot(rows_ref[...], grad, preferred_element_type=jnp.float32)
        enc_buffer[step % 2] = enc * scale
        copies(step)[0].start()
    for step in range(max(steps - 2, 0), steps):
        for copy in copies(step):
            copy.wait()


def weight_gradients(all_rows, entries, energy, own, column, row, dec, early, middle, encoded, pieces):
    coded, slope, rows = encoded
    columns = rows.shape[0]
    latents, width = dec.shape
    pieces, cuts = cut_pieces(pieces)
    count = sum(size for _, size in cuts)
    tile = min(512, latents)
    middle = [x for kind in zip(*middle, strict=True) for x in kind]
    args = [column, row, held(dec), *early, rows, coded, slope, *middle, *pieces]
    return kernel_call(
        functools.partial(last_body, cuts, len(middle) // 4, tile, all_rows, entries),
        [energy, own, *args],
        [IN_VMEM, IN_SMEM] + [IN_VMEM] * len(args),
        [pltpu.HBM((columns, latents), jnp.float32), pltpu.HBM((latents, columns), jnp.float32)],
        [
            pltpu.VMEM((2, columns, tile), jnp.float32),
            pltpu.VMEM((2, tile, columns), jnp.float32),
            pltpu.VMEM((count, width), jnp.bfloat16),
            pltpu.VMEM((count, columns), jnp.bfloat16),
            pltpu.SemaphoreType.DMA((2, 2)),
        ],
        [IN_HBM, IN_HBM],
        flops=2 * count * width * latents + 4 * count * columns * latents,
        limit=16,
    )


def bits(size):
    found, bit = [], 1
    while bit < size:
        found.append(bit)
        bit *= 2
    return found


def swap(x, even, odd=None):
    count = lax.axis_size("dp") * lax.axis_size("latent")
    odd = even if odd is None else odd
    return lax.ppermute(
        x, ("dp", "latent"), [(i, i ^ (odd if i & 1 else even)) for i in range(count)]
    )


def line_steps():
    steps = bits(lax.axis_size("latent"))[1:]
    return list(zip(steps[::-1], steps, strict=True))


def plane_steps():
    latent_size = lax.axis_size("latent")
    steps = [bit * latent_size for bit in bits(lax.axis_size("dp"))]
    return list(zip(steps, steps[::-1], strict=True))


def after(value, *done):
    return lax.optimization_barrier((value, *done))[0]


def after(value, *done):
    return lax.optimization_barrier((value, *done))[0]


def send_body(group_bits, own_ref, shuffle_ref, rows_ref, *outs):
    count, width = rows_ref.shape
    per_peer = outs[0].shape[0]
    goes_to = lax.shift_right_logical(shuffle_ref[...], group_bits) ^ own_ref[0]
    slot = shuffle_ref[...] & (count - 1)
    over_lanes = (((1,), (1,)), ((), ()))
    sublane = lax.broadcasted_iota(jnp.int32, (count, count), 0)
    lane = lax.broadcasted_iota(jnp.int32, (count, count), 1)
    peer_row = jnp.broadcast_to(goes_to, (count, count)).astype(jnp.float32)
    one_hot = (sublane == lane).astype(jnp.bfloat16)
    peer_column = lax.dot_general(
        one_hot, peer_row.astype(jnp.bfloat16), over_lanes, preferred_element_type=jnp.float32
    )
    before = (peer_column == peer_row) & (sublane < lane)
    rank = jnp.sum(before.astype(jnp.float32), axis=0, keepdims=True)
    order = goes_to.astype(jnp.float32) * per_peer + rank
    pick = (order == sublane.astype(jnp.float32)).astype(jnp.bfloat16)
    rows = jnp.dot(pick, rows_ref[...], preferred_element_type=jnp.float32)
    slot_rows = jnp.broadcast_to(slot, (128, count)).astype(jnp.float32).astype(jnp.bfloat16)
    slots = lax.dot_general(pick, slot_rows, over_lanes, preferred_element_type=jnp.float32)
    for peer, out in enumerate(outs):
        here = slice(peer * per_peer, (peer + 1) * per_peer)
        out[:, :width] = rows[here]
        out[:, width:] = slots[here]


def place_body(*refs):
    *pieces, out_ref, rows = refs
    join(pieces, rows)
    width = out_ref.shape[1]
    index = lax.broadcasted_iota(jnp.int32, (rows.shape[0], rows.shape[0]), 1).astype(jnp.float32)
    pick = (rows[:, width : width + 1] == index).astype(jnp.bfloat16)
    out_ref[...] = lax.dot_general(
        pick, rows[:, :width].astype(jnp.bfloat16), (((0,), (0,)), ((), ())), preferred_element_type=jnp.float32
    ).astype(jnp.bfloat16)


def send_rows(own, rows, shuffle):
    data_size = lax.axis_size("dp")
    latent_size = lax.axis_size("latent")
    count, width = rows.shape
    out = float_array(count // data_size, width + 128)
    body = functools.partial(send_body, len(bits(count * latent_size)))
    specs = [IN_SMEM, IN_VMEM, IN_VMEM]
    sent = kernel_call(body, [own, shuffle, rows], specs, [out] * data_size, limit=4)
    return [swap(x, peer * latent_size) if peer else x for peer, x in enumerate(sent)]


def place_rows(arrived, count, width):
    scratch = [pltpu.VMEM((count, width + 128), jnp.float32)]
    specs = [IN_VMEM] * len(arrived)
    return kernel_call(place_body, arrived, specs, [half_array(count, width)], scratch, limit=4)[0]


def shards(
    queries,
    cache_keys,
    cache_values,
    positions,
    shuffle,
    enc_weight,
    enc_bias,
    dec_weight,
    dec_bias,
):
    rows_here = queries.shape[0]
    att_width = queries.shape[1]
    data_size = lax.axis_size("dp")
    latent_size = lax.axis_size("latent")
    all_rows = rows_here * data_size * latent_size
    columns = att_width // data_size
    entries = all_rows * att_width
    core = (1, 1)
    line, plane = line_steps(), plane_steps()
    own = lax.axis_index("dp").astype(jnp.int32).reshape(1)
    bias, out_bias, places, own = lax.optimization_barrier(
        (enc_bias[None, :], dec_bias[None, :], shuffle[None, :], own)
    )
    heads_out, energy, enc = attend(queries, cache_keys, cache_values, positions, after(enc_weight, bias, out_bias, places, own))

    small_steps = plane + [core] + line
    rows = heads_out
    for number, mask in enumerate(line):
        arrived = swap(rows, *mask)
        count = len(plane) if number == 0 else 1
        if number == len(line) - 1:
            count = len(small_steps)
        for small in small_steps[:count]:
            other = swap(energy, *small)
            if small == line[0]:
                dec = load(after(dec_weight, energy))
                other = after(other, dec)
            energy = add(energy, other)
        small_steps = small_steps[count:]
        rows = joined(rows, after(arrived, energy))
        if number == 0:
            pair = rows

    def chunks(near, far, first, size, largest=256):
        step = min(size, largest)
        return [[(near, i, step), (far, i, step)] for i in range(first, first + size, step)]

    hop = swap(rows, *plane[0])
    group = whole([rows, swap(rows, *core)])
    *first_set, keep, send = encode_and_rebuild(entries, energy, own, enc, bias, dec, group, columns)
    encoded = [first_set]

    def encode_next(parts, now):
        parts = [(after(part, now), *cut) for part, *cut in parts]
        encoded.append(encode(entries, energy, own, enc, bias, parts, columns))
        return encoded[-1][0]

    arrived = swap(after(send, hop), *core)
    total = keep
    far = [rows, hop]
    for number, mask in enumerate(line[::-1]):
        last = number == len(line) - 1
        total, sent = (add_both if last else add_split)(total, arrived)
        arrived = swap(sent, *mask)
        if number == 0:
            hop = after(hop, sent)
            arrived = after(arrived, encode_next(whole([hop, swap(hop, *core)]), sent))
            for step in plane[1:2]:
                far.append(swap(joined(*(after(piece, sent) for piece in far), halves=True), *step))
        if last:
            norms_column, norms_row = decoder_norms(after(dec, sent))
            arrived = after(arrived, norms_row, far[-1])
    rebuilt_own, rows = pair_residual(entries, total, arrived, out_bias, pair, energy)
    for step in plane[2:]:
        far.append(swap(joined(*(after(piece, rows) for piece in far), halves=True), *step))
    others = [swap(after(piece, rows), *core) for piece in far[2:]]

    for mask in line[1:-1]:
        rows = joined(rows, swap(rows, *mask))
    near, late = [rows], [swap(rows, *line[-1])]
    near.append(swap(rows, *plane[0]))
    moved = send_rows(own, after(rebuilt_own, rows), places)
    waiting = []
    for piece, other in zip(far[2:], others, strict=True):
        half = piece.shape[0] // 2
        waiting += chunks(piece, other, 0, half) + chunks(piece, other, half, half)
    done = [encode_next(parts, rows) for parts in waiting[:-1]]
    late[0] = after(late[0], near[1], *done, *moved)
    grads = []

    def pre(sets, now):
        slopes = [code[1] for code in encoded[len(grads) : len(grads) + len(sets)]]
        sets = [[(after(part, now), *cut) for part, *cut in parts] for parts in sets]
        grads.extend(pre_gradient(all_rows, own, dec, norms_row, slopes, sets, columns))
        return grads[-1][0]

    def ready(sets):
        chosen = [(encoded[i], grads[i]) for i in sets]
        return [(code[2], grad[0], code[0], grad[1]) for code, grad in chosen]

    late.append(swap(late[0], *plane[0]))
    near.append(swap(joined(*near), *plane[1]))
    rows = joined(near[0], late[0])
    done = pre([whole([rows, swap(rows, *core)])], rows)
    near[2] = after(near[2], done)
    hop = joined(near[1], after(late[1], done, encode_next(waiting[-1], rows)))
    sets = [whole([hop, swap(hop, *core)])]
    for number, step in enumerate(plane[1:], 1):
        if number > 1:
            near.append(swap(joined(*near), *step))
        late.append(swap(joined(*late), *step))
        sets += chunks(near[-1], swap(near[-1], *core), 0, near[-1].shape[0])
        if number < len(plane) - 1:
            sets += chunks(late[-1], swap(late[-1], *core), 0, late[-1].shape[0])
    for first in range(0, len(sets) - 2, 2):
        done = pre(sets[first : first + 2], hop)
    count = len(grads)
    sets = [[(after(part, hop), *cut) for part, *cut in parts] for parts in sets[count - 1 :]]
    early = early_sums(all_rows, own, dec, norms_row, encoded[: count + len(sets)], grads, sets)
    count += len(sets)
    grads += [None] * len(sets)
    last = after(late[-1], early[0])
    sets = chunks(last, swap(last, *core), 0, last.shape[0])
    for parts in sets[:-1]:
        pre([parts], last)
    grad_enc, grad_dec = weight_gradients(
        all_rows,
        entries,
        energy,
        own,
        norms_column,
        norms_row,
        dec,
        early,
        ready(range(count, len(grads))),
        encoded[-1],
        sets[-1],
    )
    rebuilt = place_rows([after(part, early[0]) for part in moved], rows_here, att_width)
    return (rebuilt, grad_enc, grad_dec)


def solution(mesh):
    in_specs = (
        P(("dp", "latent"), None),
        P(("dp", "latent"), None, None),
        P(("dp", "latent"), None, None),
        P(("dp", "latent")),
        P(("dp", "latent")),
        P(None, "latent"),
        P("latent"),
        P("latent", None),
        P(),
    )
    out_specs = (P(("dp", "latent"), None), P("dp", "latent"), P("latent", "dp"))
    return jax.shard_map(shards, mesh=mesh, in_specs=in_specs, out_specs=out_specs, check_vma=False)
```

```python
import functools

import jax
import jax.numpy as jnp
from jax import lax
from jax.experimental import pallas as pl
from jax.experimental.pallas import tpu as pltpu
from jax.sharding import PartitionSpec as P

HEAD_DIM = 256


sharpness = 4.0
sparsity_weight = 1.0
epsilon = 1e-06

MIB = 1024 * 1024
LOG2E = 1.4426950408889634
IN_VMEM = pl.BlockSpec(memory_space=pltpu.VMEM)
IN_HBM = pl.BlockSpec(memory_space=pltpu.HBM)
IN_SMEM = pl.BlockSpec(memory_space=pltpu.SMEM)


def kernel_call(body, args, specs, outs, scratch=(), out_specs=None, flops=0, limit=12):
    return pl.pallas_call(
        body,
        in_specs=specs,
        out_specs=out_specs or [IN_VMEM] * len(outs),
        out_shape=outs,
        scratch_shapes=list(scratch),
        compiler_params=pltpu.CompilerParams(vmem_limit_bytes=limit * MIB),
        cost_estimate=pl.CostEstimate(flops=flops, bytes_accessed=0, transcendentals=0),
    )(*args)


def held(x):
    return pltpu.with_memory_space_constraint(x, pltpu.VMEM)


def half_array(*shape):
    return jax.ShapeDtypeStruct(shape, jnp.bfloat16)


def float_array(*shape):
    return jax.ShapeDtypeStruct(shape, jnp.float32)


def attend_body(
    kv_heads, positions_ref, queries, keys, values, heads_ref, energy_ref, q, k, v, sems
):
    rows, width = q.shape
    per_head = width // kv_heads // HEAD_DIM
    whole = pltpu.make_async_copy(queries, q, sems.at[2 * kv_heads])
    whole.start()
    copies = []
    for g in range(kv_heads):
        here = pl.ds(g * HEAD_DIM, HEAD_DIM)
        copies.append(pltpu.make_async_copy(keys.at[0, :, here], k.at[:, here], sems.at[2 * g]))
        copies.append(pltpu.make_async_copy(values.at[0, :, here], v.at[:, here], sems.at[2 * g + 1]))
    for copy in copies:
        copy.start()
    whole.wait()
    shape = (rows, keys.shape[1])
    row_index = lax.broadcasted_iota(jnp.int32, shape, 0)
    visible = lax.broadcasted_iota(jnp.int32, shape, 1) <= positions_ref[0] + row_index
    visible = jnp.concatenate([visible] * per_head, axis=0)
    energy = jnp.zeros((1, 128), jnp.float32)
    heads = [slice(i * HEAD_DIM, (i + 1) * HEAD_DIM) for i in range(kv_heads * per_head)]
    scores, probs = [], []
    for g in range(kv_heads):
        grouped = jnp.concatenate([q[:, head] for head in heads[g * per_head : (g + 1) * per_head]], axis=0)
        copies[2 * g].wait()
        product = lax.dot_general(
            grouped, k[:, heads[g]], (((1,), (1,)), ((), ())), preferred_element_type=jnp.float32
        )
        scores.append(jnp.where(visible, product * HEAD_DIM ** (-0.5), -jnp.inf))
    for score in scores:
        weight = jnp.exp(score - jnp.max(score, axis=1, keepdims=True))
        probs.append((weight / jnp.sum(weight, axis=1, keepdims=True)).astype(jnp.bfloat16))
    for g in range(kv_heads):
        copies[2 * g + 1].wait()
    for g in range(kv_heads):
        mix = jnp.dot(probs[g], v[:, heads[g]], preferred_element_type=jnp.float32).astype(jnp.bfloat16)
        for i, head in enumerate(heads[g * per_head : (g + 1) * per_head]):
            part = mix[i * rows : (i + 1) * rows]
            heads_ref[:, head] = part
            square = jnp.sum(jnp.square(part.astype(jnp.float32)), axis=0, keepdims=True)
            for lane in range(0, HEAD_DIM, 128):
                energy = energy + square[:, lane : lane + 128]
    energy_ref[...] = energy


def attend(queries, cache_keys, cache_values, positions):
    rows, width = queries.shape
    slots, kv_width = cache_keys.shape[1:]
    kv_heads = kv_width // HEAD_DIM
    hbm = [pltpu.with_memory_space_constraint(x, pltpu.HBM) for x in (queries, cache_keys, cache_values)]
    return kernel_call(
        functools.partial(attend_body, kv_heads),
        [positions, *hbm],
        [IN_SMEM] + [IN_HBM] * 3,
        [half_array(rows, width), float_array(1, 128)],
        [
            pltpu.VMEM((rows, width), jnp.bfloat16),
            pltpu.VMEM((slots, kv_width), jnp.bfloat16),
            pltpu.VMEM((slots, kv_width), jnp.bfloat16),
            pltpu.SemaphoreType.DMA((2 * kv_heads + 1,)),
        ],
        flops=4 * rows * slots * width,
    )


def load_body(parts, first, source, target, sems):
    size = source.shape[0] // parts
    columns = pl.ds(first, target.shape[1])
    copies = []
    for part in range(parts):
        here = pl.ds(part * size, size)
        copies.append(pltpu.make_async_copy(source.at[here, columns], target.at[here], sems.at[part]))
    for copy in copies:
        copy.start()
    for copy in copies:
        copy.wait()


def load(x, first, columns, parts=8):
    source = pltpu.with_memory_space_constraint(x, pltpu.HBM)
    return kernel_call(
        functools.partial(load_body, parts, first),
        [source],
        [IN_HBM],
        [pltpu.VMEM((x.shape[0], columns), x.dtype)],
        [pltpu.SemaphoreType.DMA((parts,))],
    )[0]


def norms_body(block, dec_ref, column_ref, row_ref):
    for first in range(0, dec_ref.shape[0], block):
        here = slice(first, first + block)
        square = jnp.square(dec_ref[here, :].astype(jnp.float32))
        norms = jnp.sqrt(jnp.sum(square, axis=1, keepdims=True) + epsilon)
        column_ref[here, :] = norms
        row_ref[:, here] = jnp.broadcast_to(norms, (block, 128)).T[:1]


def decoder_norms(dec):
    latents = dec.shape[0]
    return kernel_call(
        functools.partial(norms_body, 256),
        [held(dec)],
        [IN_VMEM],
        [float_array(latents, 1), float_array(1, latents)],
    )


def codes(scaled):
    decay = jnp.exp2(-jnp.abs(scaled))
    small = decay * (LOG2E - (0.5 * LOG2E) * decay)
    soft = jnp.maximum(scaled, 0.0) + jnp.where(decay < 1e-3, small, jnp.log2(1.0 + decay))
    slope = jnp.exp2(scaled - soft)
    return soft * (1.0 / (sharpness * LOG2E)), slope.astype(jnp.bfloat16)


def norm_scale(energy_ref, entries):
    return lax.rsqrt(jnp.sum(energy_ref[...], axis=1, keepdims=True) / entries + epsilon)


def add_body(a_ref, b_ref, sum_ref):
    sum_ref[...] = a_ref[...] + b_ref[...]


def add(a, b):
    return kernel_call(add_body, [a, b], [IN_VMEM] * 2, [float_array(*a.shape)], limit=4)[0]


def join_body(halves, *refs):
    *pieces, out = refs
    if not halves:
        join(pieces, out)
        return
    cuts = [(first, piece.shape[0] // 2) for first in (0, 1) for piece in pieces]
    join(pieces * 2, out, [(first * size, size) for first, size in cuts])


def joined(*pieces, halves=False):
    count = sum(piece.shape[0] for piece in pieces)
    out = [half_array(count, pieces[0].shape[1])]
    body = functools.partial(join_body, halves)
    limit = 4 + max(0, count - 256) // 64
    return kernel_call(body, pieces, [IN_VMEM] * len(pieces), out, limit=limit)[0]


def add_split_body(a_ref, b_ref, keep_ref, send_ref):
    half = keep_ref.shape[0]
    keep_ref[...] = a_ref[:half] + b_ref[:half].astype(jnp.float32)
    send_ref[...] = (a_ref[half:] + b_ref[half:].astype(jnp.float32)).astype(jnp.bfloat16)


def add_split(a, b):
    half, width = a.shape[0] // 2, a.shape[1]
    outs = [float_array(half, width), half_array(half, width)]
    return kernel_call(add_split_body, [a, b], [IN_VMEM] * 2, outs, limit=4)


def add_both_body(a_ref, b_ref, sum_ref, send_ref):
    total = a_ref[...] + b_ref[...].astype(jnp.float32)
    sum_ref[...] = total
    send_ref[...] = total.astype(jnp.bfloat16)


def add_both(a, b):
    outs = [float_array(*a.shape), half_array(*a.shape)]
    return kernel_call(add_both_body, [a, b], [IN_VMEM] * 2, outs, limit=4)


def residual_body(entries, a_ref, b_ref, bias_ref, heads_ref, energy_ref, rebuilt_ref, residual_ref):
    half = rebuilt_ref.shape[0]
    scale = norm_scale(energy_ref, entries)
    for here, there in ((slice(0, half), slice(half, 2 * half)), (slice(half, 2 * half), slice(0, half))):
        rebuilt = a_ref[here] + b_ref[there].astype(jnp.float32) + bias_ref[...]
        inputs = (heads_ref[here].astype(jnp.float32) * scale).astype(jnp.bfloat16)
        residual_ref[here] = (rebuilt - inputs.astype(jnp.float32)).astype(jnp.bfloat16)
        if here.start == 0:
            rebuilt_ref[...] = rebuilt.astype(jnp.bfloat16)


def pair_residual(entries, *args):
    count, width = args[0].shape
    body = functools.partial(residual_body, entries)
    return kernel_call(body, args, [IN_VMEM] * 5, [half_array(count // 2, width), half_array(count, width)], limit=6)


def own_columns(x, own_ref, columns):
    return x[:, pl.ds(pl.multiple_of(own_ref[0] * columns, 128), columns)]


def join(pieces, rows, cuts=None):
    start = 0
    for piece, (first, size) in zip(pieces, cuts or [(0, piece.shape[0]) for piece in pieces], strict=True):
        rows[start : start + size] = piece[first : first + size]
        start += size


def whole(parts):
    return [(part, 0, part.shape[0]) for part in parts]


def encode_body(cuts, tile, entries, energy_ref, own_ref, left_ref, right_ref, bias_ref, *refs):
    count = len(cuts)
    pieces, (codes_ref, slope_ref, part_ref), (rows, *rest) = refs[:count], refs[count : count + 3], refs[count + 3 :]
    if rest:
        dec_ref, keep_ref, send_ref, rows, coded_ref = rows, *rest
    join(pieces, rows, cuts)
    factor = sharpness * LOG2E
    scale = norm_scale(energy_ref, entries) * factor
    half = left_ref.shape[1]
    for first in range(0, 2 * half, tile):
        here = slice(first, first + tile)
        side, there = (left_ref, here) if first < half else (right_ref, slice(first - half, first - half + tile))
        product = jnp.dot(rows[...], side[:, there], preferred_element_type=jnp.float32)
        coded, slope = codes(product * scale + bias_ref[:, here] * factor)
        codes_ref[here, :] = coded.T.astype(jnp.bfloat16)
        slope_ref[:, here] = slope
        if rest:
            coded_ref[:, here] = coded.astype(jnp.bfloat16)
    part = own_columns(rows, own_ref, part_ref.shape[0])
    part_ref[...] = part.astype(jnp.float32).T.astype(jnp.bfloat16)
    if rest:
        half = keep_ref.shape[0]
        for first in range(0, dec_ref.shape[1], tile):
            here = slice(first, first + tile)
            total = jnp.dot(coded_ref[...], dec_ref[:, here], preferred_element_type=jnp.float32)
            keep_ref[:, here] = total[:half]
            send_ref[:, here] = total[half:].astype(jnp.bfloat16)


def cut_pieces(parts):
    return [part for part, _, _ in parts], [(first, size) for _, first, size in parts]


def encode(entries, energy, own, enc, bias, pieces, columns):
    width, latents = enc[0].shape[0], 2 * enc[0].shape[1]
    pieces, cuts = cut_pieces(pieces)
    count = sum(size for _, size in cuts)
    return kernel_call(
        functools.partial(encode_body, cuts, min(512, latents // 2), entries),
        [energy, own, *(held(x) for x in enc), bias, *pieces],
        [IN_VMEM, IN_SMEM] + [IN_VMEM] * (3 + len(pieces)),
        [half_array(latents, count), half_array(count, latents), half_array(columns, count)],
        [pltpu.VMEM((count, width), jnp.bfloat16)],
        flops=2 * count * width * latents,
    )


def rebuild_body(cuts, tile, entries, energy_ref, own_ref, left_ref, right_ref, bias_ref, dec_ref, *refs):
    count = len(cuts)
    pieces, outs, scratch = refs[:count], refs[count : count + 5], refs[count + 5 :]
    encode_body(
        cuts, tile, entries, energy_ref, own_ref, left_ref, right_ref, bias_ref, *pieces, *outs[:3], dec_ref, *outs[3:], *scratch
    )


def encode_and_rebuild(entries, energy, own, enc, bias, dec, pieces, columns):
    width, latents = enc[0].shape[0], 2 * enc[0].shape[1]
    pieces, cuts = cut_pieces(pieces)
    count = sum(size for _, size in cuts)
    return kernel_call(
        functools.partial(rebuild_body, cuts, min(512, latents // 2), entries),
        [energy, own, *(held(x) for x in enc), bias, held(dec), *pieces],
        [IN_VMEM, IN_SMEM] + [IN_VMEM] * (4 + len(pieces)),
        [
            half_array(latents, count),
            half_array(count, latents),
            half_array(columns, count),
            float_array(count // 2, width),
            half_array(count // 2, width),
        ],
        [pltpu.VMEM((count, width), jnp.bfloat16), pltpu.VMEM((count, latents), jnp.bfloat16)],
        flops=4 * count * width * latents,
    )


def pre_tile(rows, dec_ref, norms_ref, slope_ref, here, all_rows):
    product = lax.dot_general(
        rows[...], dec_ref[here, :], (((1,), (1,)), ((), ())), preferred_element_type=jnp.float32
    )
    grad = product * (2.0 / all_rows) + norms_ref[:, here] * (sparsity_weight / all_rows)
    return (grad * slope_ref[:, here].astype(jnp.float32)).astype(jnp.bfloat16)


def slope_body(cuts, tile, all_rows, own_ref, dec_ref, norms_ref, *refs):
    sets = len(cuts)
    slopes, refs = refs[:sets], refs[sets:]
    pieces = []
    for chosen in cuts:
        pieces.append(refs[: len(chosen)])
        refs = refs[len(chosen) :]
    grads, parts, scratch = refs[:sets], refs[sets : 2 * sets], refs[2 * sets :]
    for chosen, slope_ref, piece, grad_ref, part_ref, rows in zip(
        cuts, slopes, pieces, grads, parts, scratch, strict=True
    ):
        join(piece, rows, chosen)
        for first in range(0, dec_ref.shape[0], tile):
            here = slice(first, first + tile)
            grad_ref[:, here] = pre_tile(rows, dec_ref, norms_ref, slope_ref, here, all_rows)
        part_ref[...] = own_columns(rows, own_ref, part_ref.shape[1])


def pre_gradient(all_rows, own, dec, norms, slopes, sets, columns):
    latents, width = dec.shape
    cut_sets = [cut_pieces(pieces) for pieces in sets]
    counts = [sum(size for _, size in cuts) for _, cuts in cut_sets]
    args = [held(dec), norms, *slopes, *(part for parts, _ in cut_sets for part in parts)]
    outs = kernel_call(
        functools.partial(slope_body, [cuts for _, cuts in cut_sets], min(512, latents), all_rows),
        [own, *args],
        [IN_SMEM] + [IN_VMEM] * len(args),
        [half_array(count, latents) for count in counts] + [half_array(count, columns) for count in counts],
        [pltpu.VMEM((count, width), jnp.bfloat16) for count in counts],
        flops=2 * sum(counts) * width * latents,
        limit=12 + max(0, sum(counts) - 512) // 32,
    )
    return list(zip(outs[: len(sets)], outs[len(sets) :], strict=True))


def early_body(cuts, given, tile, all_rows, own_ref, dec_ref, norms_ref, *refs):
    sets = len(cuts)
    rows, coded, slopes, refs = refs[: sets + given], refs[sets + given : 2 * (sets + given)], refs[2 * (sets + given) :][:sets], refs[2 * (sets + given) + sets :]
    grads, parts, refs = refs[:given], refs[given : 2 * given], refs[2 * given :]
    pieces = []
    for chosen in cuts:
        pieces.append(refs[: len(chosen)])
        refs = refs[len(chosen) :]
    (enc_ref, dec_sum, sums_ref), scratch = refs[:3], refs[3:]
    residuals, own_parts = scratch[:sets], scratch[sets:]
    for chosen, piece, residual, part in zip(cuts, pieces, residuals, own_parts, strict=True):
        join(piece, residual, chosen)
        part[...] = own_columns(residual, own_ref, part.shape[1])
    for first in range(0, dec_ref.shape[0], tile):
        here = slice(first, first + tile)
        made = [
            pre_tile(residual, dec_ref, norms_ref, slope_ref, here, all_rows)
            for residual, slope_ref in zip(residuals, slopes, strict=True)
        ]
        enc, dec, sums = 0.0, 0.0, 0.0
        for rows_set, grad in zip(rows, [grad[:, here] for grad in grads] + made, strict=True):
            enc = enc + jnp.dot(rows_set[...], grad, preferred_element_type=jnp.float32)
        for coded_set, part in zip(coded, (*parts, *own_parts), strict=True):
            dec = dec + jnp.dot(coded_set[here, :], part[...], preferred_element_type=jnp.float32)
            sums = sums + jnp.sum(coded_set[here, :].astype(jnp.float32), axis=1, keepdims=True)
        enc_ref[:, here] = enc
        dec_sum[here, :] = dec
        sums_ref[here, :] = sums


def early_sums(all_rows, own, dec, norms, encoded, grads, sets):
    latents, width = dec.shape
    columns = encoded[0][2].shape[0]
    cut_sets = [cut_pieces(pieces) for pieces in sets]
    counts = [sum(size for _, size in cuts) for _, cuts in cut_sets]
    args = [held(dec), norms, *(x[2] for x in encoded), *(x[0] for x in encoded)]
    args += [x[1] for x in encoded[len(grads) :]] + [x[0] for x in grads] + [x[1] for x in grads]
    args += [part for parts, _ in cut_sets for part in parts]
    return kernel_call(
        functools.partial(early_body, [cuts for _, cuts in cut_sets], len(grads), min(512, latents), all_rows),
        [own, *args],
        [IN_SMEM] + [IN_VMEM] * len(args),
        [float_array(columns, latents), float_array(latents, columns), float_array(latents, 1)],
        [pltpu.VMEM((count, width), jnp.bfloat16) for count in counts]
        + [pltpu.VMEM((count, columns), jnp.bfloat16) for count in counts],
        flops=2 * sum(counts) * width * latents,
        limit=16 + max(0, sum(counts) - 512) // 32,
    )


def last_body(
    cuts, groups, tile, all_rows, entries, energy_ref, own_ref, column_ref, row_ref, dec_ref, enc_sum, dec_sum,
    sums_ref, rows_ref, coded_ref, slope_ref, *refs,
):
    rows, grads, coded, parts = (refs[i * groups : (i + 1) * groups] for i in range(4))
    refs = refs[4 * groups :]
    count = len(cuts)
    pieces, (enc_out, dec_out, enc_buffer, dec_buffer, residual, part, sems) = refs[:count], refs[count:]
    columns = dec_buffer.shape[2]
    steps = dec_ref.shape[0] // tile
    scale = norm_scale(energy_ref, entries)
    join(pieces, residual, cuts)
    part[...] = own_columns(residual, own_ref, columns)

    def copies(step):
        slot, here = step % 2, pl.ds(step * tile, tile)
        return (
            pltpu.make_async_copy(enc_buffer.at[slot], enc_out.at[:, here], sems.at[slot, 0]),
            pltpu.make_async_copy(dec_buffer.at[slot], dec_out.at[here], sems.at[slot, 1]),
        )

    for step in range(steps):
        if step >= 2:
            for copy in copies(step - 2):
                copy.wait()
        here = slice(step * tile, (step + 1) * tile)
        enc, dec, sums = enc_sum[:, here], dec_sum[here, :], sums_ref[here, :]
        for coded_set, part_set in zip((*coded, coded_ref), (*parts, part), strict=True):
            dec = dec + jnp.dot(coded_set[here, :], part_set[...], preferred_element_type=jnp.float32)
            sums = sums + jnp.sum(coded_set[here, :].astype(jnp.float32), axis=1, keepdims=True)
        weights = own_columns(dec_ref.at[here, :], own_ref, columns).astype(jnp.float32)
        factor = sums / column_ref[here, :] * (sparsity_weight / all_rows)
        dec_buffer[step % 2] = dec * (2.0 / all_rows) + factor * weights
        copies(step)[1].start()
        for rows_set, grad in zip(rows, grads, strict=True):
            enc = enc + jnp.dot(rows_set[...], grad[:, here], preferred_element_type=jnp.float32)
        grad = pre_tile(residual, dec_ref, row_ref, slope_ref, here, all_rows)
        enc = enc + jnp.dot(rows_ref[...], grad, preferred_element_type=jnp.float32)
        enc_buffer[step % 2] = enc * scale
        copies(step)[0].start()
    for step in range(max(steps - 2, 0), steps):
        for copy in copies(step):
            copy.wait()


def weight_gradients(all_rows, entries, energy, own, column, row, dec, early, middle, encoded, pieces):
    coded, slope, rows = encoded
    columns = rows.shape[0]
    latents, width = dec.shape
    pieces, cuts = cut_pieces(pieces)
    count = sum(size for _, size in cuts)
    tile = min(512, latents)
    middle = [x for kind in zip(*middle, strict=True) for x in kind]
    args = [column, row, held(dec), *early, rows, coded, slope, *middle, *pieces]
    return kernel_call(
        functools.partial(last_body, cuts, len(middle) // 4, tile, all_rows, entries),
        [energy, own, *args],
        [IN_VMEM, IN_SMEM] + [IN_VMEM] * len(args),
        [pltpu.HBM((columns, latents), jnp.float32), pltpu.HBM((latents, columns), jnp.float32)],
        [
            pltpu.VMEM((2, columns, tile), jnp.float32),
            pltpu.VMEM((2, tile, columns), jnp.float32),
            pltpu.VMEM((count, width), jnp.bfloat16),
            pltpu.VMEM((count, columns), jnp.bfloat16),
            pltpu.SemaphoreType.DMA((2, 2)),
        ],
        [IN_HBM, IN_HBM],
        flops=2 * count * width * latents + 4 * count * columns * latents,
        limit=16,
    )


def bits(size):
    found, bit = [], 1
    while bit < size:
        found.append(bit)
        bit *= 2
    return found


def swap(x, even, odd=None):
    count = lax.axis_size("dp") * lax.axis_size("latent")
    odd = even if odd is None else odd
    return lax.ppermute(
        x, ("dp", "latent"), [(i, i ^ (odd if i & 1 else even)) for i in range(count)]
    )


def line_steps():
    steps = bits(lax.axis_size("latent"))[1:]
    return list(zip(steps[::-1], steps, strict=True))


def plane_steps():
    latent_size = lax.axis_size("latent")
    steps = [bit * latent_size for bit in bits(lax.axis_size("dp"))]
    return list(zip(steps, steps[::-1], strict=True))


def after(value, *done):
    return lax.optimization_barrier((value, *done))[0]


def after(value, *done):
    return lax.optimization_barrier((value, *done))[0]


def send_body(group_bits, own_ref, shuffle_ref, rows_ref, *outs):
    count, width = rows_ref.shape
    per_peer = outs[0].shape[0]
    goes_to = lax.shift_right_logical(shuffle_ref[...], group_bits) ^ own_ref[0]
    slot = shuffle_ref[...] & (count - 1)
    over_lanes = (((1,), (1,)), ((), ()))
    sublane = lax.broadcasted_iota(jnp.int32, (count, count), 0)
    lane = lax.broadcasted_iota(jnp.int32, (count, count), 1)
    peer_row = jnp.broadcast_to(goes_to, (count, count)).astype(jnp.float32)
    one_hot = (sublane == lane).astype(jnp.bfloat16)
    peer_column = lax.dot_general(
        one_hot, peer_row.astype(jnp.bfloat16), over_lanes, preferred_element_type=jnp.float32
    )
    before = (peer_column == peer_row) & (sublane < lane)
    rank = jnp.sum(before.astype(jnp.float32), axis=0, keepdims=True)
    order = goes_to.astype(jnp.float32) * per_peer + rank
    pick = (order == sublane.astype(jnp.float32)).astype(jnp.bfloat16)
    rows = jnp.dot(pick, rows_ref[...], preferred_element_type=jnp.float32)
    slot_rows = jnp.broadcast_to(slot, (128, count)).astype(jnp.float32).astype(jnp.bfloat16)
    slots = lax.dot_general(pick, slot_rows, over_lanes, preferred_element_type=jnp.float32)
    for peer, out in enumerate(outs):
        here = slice(peer * per_peer, (peer + 1) * per_peer)
        out[:, :width] = rows[here]
        out[:, width:] = slots[here]


def place_body(*refs):
    *pieces, out_ref, rows = refs
    join(pieces, rows)
    width = out_ref.shape[1]
    index = lax.broadcasted_iota(jnp.int32, (rows.shape[0], rows.shape[0]), 1).astype(jnp.float32)
    pick = (rows[:, width : width + 1] == index).astype(jnp.bfloat16)
    out_ref[...] = lax.dot_general(
        pick, rows[:, :width].astype(jnp.bfloat16), (((0,), (0,)), ((), ())), preferred_element_type=jnp.float32
    ).astype(jnp.bfloat16)


def send_rows(own, rows, shuffle):
    data_size = lax.axis_size("dp")
    latent_size = lax.axis_size("latent")
    count, width = rows.shape
    out = float_array(count // data_size, width + 128)
    body = functools.partial(send_body, len(bits(count * latent_size)))
    specs = [IN_SMEM, IN_VMEM, IN_VMEM]
    sent = kernel_call(body, [own, shuffle, rows], specs, [out] * data_size, limit=4)
    return [swap(x, peer * latent_size) if peer else x for peer, x in enumerate(sent)]


def place_rows(arrived, count, width):
    scratch = [pltpu.VMEM((count, width + 128), jnp.float32)]
    specs = [IN_VMEM] * len(arrived)
    return kernel_call(place_body, arrived, specs, [half_array(count, width)], scratch, limit=4)[0]


def shards(
    queries,
    cache_keys,
    cache_values,
    positions,
    shuffle,
    enc_weight,
    enc_bias,
    dec_weight,
    dec_bias,
):
    rows_here = queries.shape[0]
    att_width = queries.shape[1]
    data_size = lax.axis_size("dp")
    latent_size = lax.axis_size("latent")
    all_rows = rows_here * data_size * latent_size
    columns = att_width // data_size
    entries = all_rows * att_width
    core = (1, 1)
    line, plane = line_steps(), plane_steps()
    own = lax.axis_index("dp").astype(jnp.int32).reshape(1)
    bias, out_bias, places, own = lax.optimization_barrier(
        (enc_bias[None, :], dec_bias[None, :], shuffle[None, :], own)
    )
    heads_out, energy = attend(after(queries, bias, out_bias, places, own), cache_keys, cache_values, positions)

    small_steps = plane + [core] + line
    enc, latents_here = [], enc_weight.shape[1]
    rows = heads_out
    for number, mask in enumerate(line):
        arrived = swap(rows, *mask)
        count = len(plane) if number == 0 else 1
        if number == len(line) - 1:
            count = len(small_steps)
        for small in small_steps[:count]:
            other = swap(energy, *small)
            if small == line[0]:
                dec = load(after(dec_weight, energy), 0, att_width)
                other = after(other, dec)
            elif small in plane[:2]:
                side = latents_here // 2
                enc.append(load(after(enc_weight, energy), len(enc) * side, side))
                other = after(other, enc[-1])
            energy = add(energy, other)
        small_steps = small_steps[count:]
        rows = joined(rows, after(arrived, energy))
        if number == 0:
            pair = rows

    def chunks(near, far, first, size, largest=256):
        step = min(size, largest)
        return [[(near, i, step), (far, i, step)] for i in range(first, first + size, step)]

    hop = swap(rows, *plane[0])
    group = whole([rows, swap(rows, *core)])
    *first_set, keep, send = encode_and_rebuild(entries, energy, own, enc, bias, dec, group, columns)
    encoded = [first_set]

    def encode_next(parts, now):
        parts = [(after(part, now), *cut) for part, *cut in parts]
        encoded.append(encode(entries, energy, own, enc, bias, parts, columns))
        return encoded[-1][0]

    arrived = swap(after(send, hop), *core)
    total = keep
    far = [rows, hop]
    for number, mask in enumerate(line[::-1]):
        last = number == len(line) - 1
        total, sent = (add_both if last else add_split)(total, arrived)
        arrived = swap(sent, *mask)
        if number == 0:
            hop = after(hop, sent)
            arrived = after(arrived, encode_next(whole([hop, swap(hop, *core)]), sent))
            for step in plane[1:2]:
                far.append(swap(joined(*(after(piece, sent) for piece in far), halves=True), *step))
        if last:
            norms_column, norms_row = decoder_norms(after(dec, sent))
            arrived = after(arrived, norms_row, far[-1])
    rebuilt_own, rows = pair_residual(entries, total, arrived, out_bias, pair, energy)
    for step in plane[2:]:
        far.append(swap(joined(*(after(piece, rows) for piece in far), halves=True), *step))
    others = [swap(after(piece, rows), *core) for piece in far[2:]]

    for mask in line[1:-1]:
        rows = joined(rows, swap(rows, *mask))
    near, late = [rows], [swap(rows, *line[-1])]
    near.append(swap(rows, *plane[0]))
    moved = send_rows(own, after(rebuilt_own, rows), places)
    waiting = []
    for piece, other in zip(far[2:], others, strict=True):
        half = piece.shape[0] // 2
        waiting += chunks(piece, other, 0, half) + chunks(piece, other, half, half)
    done = [encode_next(parts, rows) for parts in waiting[:-1]]
    late[0] = after(late[0], near[1], *done, *moved)
    grads = []

    def pre(sets, now):
        slopes = [code[1] for code in encoded[len(grads) : len(grads) + len(sets)]]
        sets = [[(after(part, now), *cut) for part, *cut in parts] for parts in sets]
        grads.extend(pre_gradient(all_rows, own, dec, norms_row, slopes, sets, columns))
        return grads[-1][0]

    def ready(sets):
        chosen = [(encoded[i], grads[i]) for i in sets]
        return [(code[2], grad[0], code[0], grad[1]) for code, grad in chosen]

    late.append(swap(late[0], *plane[0]))
    near.append(swap(joined(*near), *plane[1]))
    rows = joined(near[0], late[0])
    done = pre([whole([rows, swap(rows, *core)])], rows)
    near[2] = after(near[2], done)
    hop = joined(near[1], after(late[1], done, encode_next(waiting[-1], rows)))
    sets = [whole([hop, swap(hop, *core)])]
    for number, step in enumerate(plane[1:], 1):
        if number > 1:
            near.append(swap(joined(*near), *step))
        late.append(swap(joined(*late), *step))
        sets += chunks(near[-1], swap(near[-1], *core), 0, near[-1].shape[0])
        if number < len(plane) - 1:
            sets += chunks(late[-1], swap(late[-1], *core), 0, late[-1].shape[0])
    for first in range(0, len(sets) - 2, 2):
        done = pre(sets[first : first + 2], hop)
    count = len(grads)
    sets = [[(after(part, hop), *cut) for part, *cut in parts] for parts in sets[count - 1 :]]
    early = early_sums(all_rows, own, dec, norms_row, encoded[: count + len(sets)], grads, sets)
    count += len(sets)
    grads += [None] * len(sets)
    last = after(late[-1], early[0])
    sets = chunks(last, swap(last, *core), 0, last.shape[0])
    for parts in sets[:-1]:
        pre([parts], last)
    grad_enc, grad_dec = weight_gradients(
        all_rows,
        entries,
        energy,
        own,
        norms_column,
        norms_row,
        dec,
        early,
        ready(range(count, len(grads))),
        encoded[-1],
        sets[-1],
    )
    rebuilt = place_rows([after(part, early[0]) for part in moved], rows_here, att_width)
    return (rebuilt, grad_enc, grad_dec)


def solution(mesh):
    in_specs = (
        P(("dp", "latent"), None),
        P(("dp", "latent"), None, None),
        P(("dp", "latent"), None, None),
        P(("dp", "latent")),
        P(("dp", "latent")),
        P(None, "latent"),
        P("latent"),
        P("latent", None),
        P(),
    )
    out_specs = (P(("dp", "latent"), None), P("dp", "latent"), P("latent", "dp"))
    return jax.shard_map(shards, mesh=mesh, in_specs=in_specs, out_specs=out_specs, check_vma=False)
```

```python
import functools

import jax
import jax.numpy as jnp
from jax import lax
from jax.experimental import pallas as pl
from jax.experimental.pallas import tpu as pltpu
from jax.sharding import PartitionSpec as P

HEAD_DIM = 256


sharpness = 4.0
sparsity_weight = 1.0
epsilon = 1e-06

MIB = 1024 * 1024
LOG2E = 1.4426950408889634
IN_VMEM = pl.BlockSpec(memory_space=pltpu.VMEM)
IN_HBM = pl.BlockSpec(memory_space=pltpu.HBM)
IN_SMEM = pl.BlockSpec(memory_space=pltpu.SMEM)


def kernel_call(body, args, specs, outs, scratch=(), out_specs=None, flops=0, limit=12):
    return pl.pallas_call(
        body,
        in_specs=specs,
        out_specs=out_specs or [IN_VMEM] * len(outs),
        out_shape=outs,
        scratch_shapes=list(scratch),
        compiler_params=pltpu.CompilerParams(vmem_limit_bytes=limit * MIB),
        cost_estimate=pl.CostEstimate(flops=flops, bytes_accessed=0, transcendentals=0),
    )(*args)


def held(x):
    return pltpu.with_memory_space_constraint(x, pltpu.VMEM)


def half_array(*shape):
    return jax.ShapeDtypeStruct(shape, jnp.bfloat16)


def float_array(*shape):
    return jax.ShapeDtypeStruct(shape, jnp.float32)


def attend_body(
    kv_heads, positions_ref, queries, keys, values, heads_ref, energy_ref, q, k, v, sems
):
    rows, width = q.shape
    per_head = width // kv_heads // HEAD_DIM
    whole = pltpu.make_async_copy(queries, q, sems.at[2 * kv_heads])
    whole.start()
    copies = []
    for g in range(kv_heads):
        here = pl.ds(g * HEAD_DIM, HEAD_DIM)
        copies.append(pltpu.make_async_copy(keys.at[0, :, here], k.at[:, here], sems.at[2 * g]))
        copies.append(pltpu.make_async_copy(values.at[0, :, here], v.at[:, here], sems.at[2 * g + 1]))
    for copy in copies:
        copy.start()
    whole.wait()
    shape = (rows, keys.shape[1])
    row_index = lax.broadcasted_iota(jnp.int32, shape, 0)
    visible = lax.broadcasted_iota(jnp.int32, shape, 1) <= positions_ref[0] + row_index
    visible = jnp.concatenate([visible] * per_head, axis=0)
    energy = jnp.zeros((1, 128), jnp.float32)
    heads = [slice(i * HEAD_DIM, (i + 1) * HEAD_DIM) for i in range(kv_heads * per_head)]
    scores, probs = [], []
    for g in range(kv_heads):
        grouped = jnp.concatenate([q[:, head] for head in heads[g * per_head : (g + 1) * per_head]], axis=0)
        copies[2 * g].wait()
        product = lax.dot_general(
            grouped, k[:, heads[g]], (((1,), (1,)), ((), ())), preferred_element_type=jnp.float32
        )
        scores.append(jnp.where(visible, product * HEAD_DIM ** (-0.5), -jnp.inf))
    for score in scores:
        weight = jnp.exp(score - jnp.max(score, axis=1, keepdims=True))
        probs.append((weight / jnp.sum(weight, axis=1, keepdims=True)).astype(jnp.bfloat16))
    for g in range(kv_heads):
        copies[2 * g + 1].wait()
    for g in range(kv_heads):
        mix = jnp.dot(probs[g], v[:, heads[g]], preferred_element_type=jnp.float32).astype(jnp.bfloat16)
        for i, head in enumerate(heads[g * per_head : (g + 1) * per_head]):
            part = mix[i * rows : (i + 1) * rows]
            heads_ref[:, head] = part
            square = jnp.sum(jnp.square(part.astype(jnp.float32)), axis=0, keepdims=True)
            for lane in range(0, HEAD_DIM, 128):
                energy = energy + square[:, lane : lane + 128]
    energy_ref[...] = energy


def attend(queries, cache_keys, cache_values, positions):
    rows, width = queries.shape
    slots, kv_width = cache_keys.shape[1:]
    kv_heads = kv_width // HEAD_DIM
    hbm = [pltpu.with_memory_space_constraint(x, pltpu.HBM) for x in (queries, cache_keys, cache_values)]
    return kernel_call(
        functools.partial(attend_body, kv_heads),
        [positions, *hbm],
        [IN_SMEM] + [IN_HBM] * 3,
        [half_array(rows, width), float_array(1, 128)],
        [
            pltpu.VMEM((rows, width), jnp.bfloat16),
            pltpu.VMEM((slots, kv_width), jnp.bfloat16),
            pltpu.VMEM((slots, kv_width), jnp.bfloat16),
            pltpu.SemaphoreType.DMA((2 * kv_heads + 1,)),
        ],
        flops=4 * rows * slots * width,
    )


def load_body(parts, first, source, target, sems):
    size = source.shape[0] // parts
    columns = pl.ds(first, target.shape[1])
    copies = []
    for part in range(parts):
        here = pl.ds(part * size, size)
        copies.append(pltpu.make_async_copy(source.at[here, columns], target.at[here], sems.at[part]))
    for copy in copies:
        copy.start()
    for copy in copies:
        copy.wait()


def load(x, first, columns, parts=8):
    source = pltpu.with_memory_space_constraint(x, pltpu.HBM)
    return kernel_call(
        functools.partial(load_body, parts, first),
        [source],
        [IN_HBM],
        [pltpu.VMEM((x.shape[0], columns), x.dtype)],
        [pltpu.SemaphoreType.DMA((parts,))],
    )[0]


def norms_body(block, dec_ref, column_ref, row_ref):
    for first in range(0, dec_ref.shape[0], block):
        here = slice(first, first + block)
        square = jnp.square(dec_ref[here, :].astype(jnp.float32))
        norms = jnp.sqrt(jnp.sum(square, axis=1, keepdims=True) + epsilon)
        column_ref[here, :] = norms
        row_ref[:, here] = jnp.broadcast_to(norms, (block, 128)).T[:1]


def decoder_norms(dec):
    latents = dec.shape[0]
    return kernel_call(
        functools.partial(norms_body, 256),
        [held(dec)],
        [IN_VMEM],
        [float_array(latents, 1), float_array(1, latents)],
    )


def codes(scaled):
    decay = jnp.exp2(-jnp.abs(scaled))
    small = decay * (LOG2E - (0.5 * LOG2E) * decay)
    soft = jnp.maximum(scaled, 0.0) + jnp.where(decay < 1e-3, small, jnp.log2(1.0 + decay))
    slope = jnp.exp2(scaled - soft)
    return soft * (1.0 / (sharpness * LOG2E)), slope.astype(jnp.bfloat16)


def norm_scale(energy_ref, entries):
    return lax.rsqrt(jnp.sum(energy_ref[...], axis=1, keepdims=True) / entries + epsilon)


def add_body(a_ref, b_ref, sum_ref):
    sum_ref[...] = a_ref[...] + b_ref[...]


def add(a, b):
    return kernel_call(add_body, [a, b], [IN_VMEM] * 2, [float_array(*a.shape)], limit=4)[0]


def join_body(halves, *refs):
    *pieces, out = refs
    if not halves:
        join(pieces, out)
        return
    cuts = [(first, piece.shape[0] // 2) for first in (0, 1) for piece in pieces]
    join(pieces * 2, out, [(first * size, size) for first, size in cuts])


def joined(*pieces, halves=False):
    count = sum(piece.shape[0] for piece in pieces)
    out = [half_array(count, pieces[0].shape[1])]
    body = functools.partial(join_body, halves)
    limit = 4 + max(0, count - 256) // 64
    return kernel_call(body, pieces, [IN_VMEM] * len(pieces), out, limit=limit)[0]


def add_split_body(a_ref, b_ref, keep_ref, send_ref):
    half = keep_ref.shape[0]
    keep_ref[...] = a_ref[:half] + b_ref[:half].astype(jnp.float32)
    send_ref[...] = (a_ref[half:] + b_ref[half:].astype(jnp.float32)).astype(jnp.bfloat16)


def add_split(a, b):
    half, width = a.shape[0] // 2, a.shape[1]
    outs = [float_array(half, width), half_array(half, width)]
    return kernel_call(add_split_body, [a, b], [IN_VMEM] * 2, outs, limit=4)


def add_both_body(a_ref, b_ref, sum_ref, send_ref):
    total = a_ref[...] + b_ref[...].astype(jnp.float32)
    sum_ref[...] = total
    send_ref[...] = total.astype(jnp.bfloat16)


def add_both(a, b):
    outs = [float_array(*a.shape), half_array(*a.shape)]
    return kernel_call(add_both_body, [a, b], [IN_VMEM] * 2, outs, limit=4)


def residual_body(entries, a_ref, b_ref, bias_ref, heads_ref, energy_ref, rebuilt_ref, residual_ref):
    half = rebuilt_ref.shape[0]
    scale = norm_scale(energy_ref, entries)
    for here, there in ((slice(0, half), slice(half, 2 * half)), (slice(half, 2 * half), slice(0, half))):
        rebuilt = a_ref[here] + b_ref[there].astype(jnp.float32) + bias_ref[...]
        inputs = (heads_ref[here].astype(jnp.float32) * scale).astype(jnp.bfloat16)
        residual_ref[here] = (rebuilt - inputs.astype(jnp.float32)).astype(jnp.bfloat16)
        if here.start == 0:
            rebuilt_ref[...] = rebuilt.astype(jnp.bfloat16)


def pair_residual(entries, *args):
    count, width = args[0].shape
    body = functools.partial(residual_body, entries)
    return kernel_call(body, args, [IN_VMEM] * 5, [half_array(count // 2, width), half_array(count, width)], limit=6)


def own_columns(x, own_ref, columns):
    return x[:, pl.ds(pl.multiple_of(own_ref[0] * columns, 128), columns)]


def join(pieces, rows, cuts=None):
    start = 0
    for piece, (first, size) in zip(pieces, cuts or [(0, piece.shape[0]) for piece in pieces], strict=True):
        rows[start : start + size] = piece[first : first + size]
        start += size


def whole(parts):
    return [(part, 0, part.shape[0]) for part in parts]


def encode_body(cuts, tile, entries, energy_ref, own_ref, left_ref, right_ref, bias_ref, *refs):
    count = len(cuts)
    pieces, (codes_ref, slope_ref, part_ref), (rows, *rest) = refs[:count], refs[count : count + 3], refs[count + 3 :]
    if rest:
        dec_ref, keep_ref, send_ref, rows, coded_ref = rows, *rest
    join(pieces, rows, cuts)
    factor = sharpness * LOG2E
    scale = norm_scale(energy_ref, entries) * factor
    half = left_ref.shape[1]
    for first in range(0, 2 * half, tile):
        here = slice(first, first + tile)
        side, there = (left_ref, here) if first < half else (right_ref, slice(first - half, first - half + tile))
        product = jnp.dot(rows[...], side[:, there], preferred_element_type=jnp.float32)
        coded, slope = codes(product * scale + bias_ref[:, here] * factor)
        codes_ref[here, :] = coded.T.astype(jnp.bfloat16)
        slope_ref[:, here] = slope
        if rest:
            coded_ref[:, here] = coded.astype(jnp.bfloat16)
    part = own_columns(rows, own_ref, part_ref.shape[0])
    part_ref[...] = part.astype(jnp.float32).T.astype(jnp.bfloat16)
    if rest:
        half = keep_ref.shape[0]
        for first in range(0, dec_ref.shape[1], tile):
            here = slice(first, first + tile)
            total = jnp.dot(coded_ref[...], dec_ref[:, here], preferred_element_type=jnp.float32)
            keep_ref[:, here] = total[:half]
            send_ref[:, here] = total[half:].astype(jnp.bfloat16)


def cut_pieces(parts):
    return [part for part, _, _ in parts], [(first, size) for _, first, size in parts]


def encode(entries, energy, own, enc, bias, pieces, columns):
    width, latents = enc[0].shape[0], 2 * enc[0].shape[1]
    pieces, cuts = cut_pieces(pieces)
    count = sum(size for _, size in cuts)
    return kernel_call(
        functools.partial(encode_body, cuts, min(512, latents // 2), entries),
        [energy, own, *(held(x) for x in enc), bias, *pieces],
        [IN_VMEM, IN_SMEM] + [IN_VMEM] * (3 + len(pieces)),
        [half_array(latents, count), half_array(count, latents), half_array(columns, count)],
        [pltpu.VMEM((count, width), jnp.bfloat16)],
        flops=2 * count * width * latents,
    )


def rebuild_body(cuts, tile, entries, energy_ref, own_ref, left_ref, right_ref, bias_ref, dec_ref, *refs):
    count = len(cuts)
    pieces, outs, scratch = refs[:count], refs[count : count + 5], refs[count + 5 :]
    encode_body(
        cuts, tile, entries, energy_ref, own_ref, left_ref, right_ref, bias_ref, *pieces, *outs[:3], dec_ref, *outs[3:], *scratch
    )


def encode_and_rebuild(entries, energy, own, enc, bias, dec, pieces, columns):
    width, latents = enc[0].shape[0], 2 * enc[0].shape[1]
    pieces, cuts = cut_pieces(pieces)
    count = sum(size for _, size in cuts)
    return kernel_call(
        functools.partial(rebuild_body, cuts, min(512, latents // 2), entries),
        [energy, own, *(held(x) for x in enc), bias, held(dec), *pieces],
        [IN_VMEM, IN_SMEM] + [IN_VMEM] * (4 + len(pieces)),
        [
            half_array(latents, count),
            half_array(count, latents),
            half_array(columns, count),
            float_array(count // 2, width),
            half_array(count // 2, width),
        ],
        [pltpu.VMEM((count, width), jnp.bfloat16), pltpu.VMEM((count, latents), jnp.bfloat16)],
        flops=4 * count * width * latents,
    )


def pre_tile(rows, dec_ref, norms_ref, slope_ref, here, all_rows):
    product = lax.dot_general(
        rows[...], dec_ref[here, :], (((1,), (1,)), ((), ())), preferred_element_type=jnp.float32
    )
    grad = product * (2.0 / all_rows) + norms_ref[:, here] * (sparsity_weight / all_rows)
    return (grad * slope_ref[:, here].astype(jnp.float32)).astype(jnp.bfloat16)


def slope_body(cuts, tile, all_rows, own_ref, dec_ref, norms_ref, *refs):
    sets = len(cuts)
    slopes, refs = refs[:sets], refs[sets:]
    pieces = []
    for chosen in cuts:
        pieces.append(refs[: len(chosen)])
        refs = refs[len(chosen) :]
    grads, parts, scratch = refs[:sets], refs[sets : 2 * sets], refs[2 * sets :]
    for chosen, slope_ref, piece, grad_ref, part_ref, rows in zip(
        cuts, slopes, pieces, grads, parts, scratch, strict=True
    ):
        join(piece, rows, chosen)
        for first in range(0, dec_ref.shape[0], tile):
            here = slice(first, first + tile)
            grad_ref[:, here] = pre_tile(rows, dec_ref, norms_ref, slope_ref, here, all_rows)
        part_ref[...] = own_columns(rows, own_ref, part_ref.shape[1])


def pre_gradient(all_rows, own, dec, norms, slopes, sets, columns):
    latents, width = dec.shape
    cut_sets = [cut_pieces(pieces) for pieces in sets]
    counts = [sum(size for _, size in cuts) for _, cuts in cut_sets]
    args = [held(dec), norms, *slopes, *(part for parts, _ in cut_sets for part in parts)]
    outs = kernel_call(
        functools.partial(slope_body, [cuts for _, cuts in cut_sets], min(512, latents), all_rows),
        [own, *args],
        [IN_SMEM] + [IN_VMEM] * len(args),
        [half_array(count, latents) for count in counts] + [half_array(count, columns) for count in counts],
        [pltpu.VMEM((count, width), jnp.bfloat16) for count in counts],
        flops=2 * sum(counts) * width * latents,
        limit=12 + max(0, sum(counts) - 512) // 32,
    )
    return list(zip(outs[: len(sets)], outs[len(sets) :], strict=True))


def early_body(cuts, given, tile, all_rows, own_ref, dec_ref, norms_ref, *refs):
    sets = len(cuts)
    rows, coded, slopes, refs = refs[: sets + given], refs[sets + given : 2 * (sets + given)], refs[2 * (sets + given) :][:sets], refs[2 * (sets + given) + sets :]
    grads, parts, refs = refs[:given], refs[given : 2 * given], refs[2 * given :]
    pieces = []
    for chosen in cuts:
        pieces.append(refs[: len(chosen)])
        refs = refs[len(chosen) :]
    (enc_ref, dec_sum, sums_ref), scratch = refs[:3], refs[3:]
    residuals, own_parts = scratch[:sets], scratch[sets:]
    for chosen, piece, residual, part in zip(cuts, pieces, residuals, own_parts, strict=True):
        join(piece, residual, chosen)
        part[...] = own_columns(residual, own_ref, part.shape[1])
    for first in range(0, dec_ref.shape[0], tile):
        here = slice(first, first + tile)
        made = [
            pre_tile(residual, dec_ref, norms_ref, slope_ref, here, all_rows)
            for residual, slope_ref in zip(residuals, slopes, strict=True)
        ]
        enc, dec, sums = 0.0, 0.0, 0.0
        for rows_set, grad in zip(rows, [grad[:, here] for grad in grads] + made, strict=True):
            enc = enc + jnp.dot(rows_set[...], grad, preferred_element_type=jnp.float32)
        for coded_set, part in zip(coded, (*parts, *own_parts), strict=True):
            dec = dec + jnp.dot(coded_set[here, :], part[...], preferred_element_type=jnp.float32)
            sums = sums + jnp.sum(coded_set[here, :].astype(jnp.float32), axis=1, keepdims=True)
        enc_ref[:, here] = enc
        dec_sum[here, :] = dec
        sums_ref[here, :] = sums


def early_sums(all_rows, own, dec, norms, encoded, grads, sets):
    latents, width = dec.shape
    columns = encoded[0][2].shape[0]
    cut_sets = [cut_pieces(pieces) for pieces in sets]
    counts = [sum(size for _, size in cuts) for _, cuts in cut_sets]
    args = [held(dec), norms, *(x[2] for x in encoded), *(x[0] for x in encoded)]
    args += [x[1] for x in encoded[len(grads) :]] + [x[0] for x in grads] + [x[1] for x in grads]
    args += [part for parts, _ in cut_sets for part in parts]
    return kernel_call(
        functools.partial(early_body, [cuts for _, cuts in cut_sets], len(grads), min(512, latents), all_rows),
        [own, *args],
        [IN_SMEM] + [IN_VMEM] * len(args),
        [float_array(columns, latents), float_array(latents, columns), float_array(latents, 1)],
        [pltpu.VMEM((count, width), jnp.bfloat16) for count in counts]
        + [pltpu.VMEM((count, columns), jnp.bfloat16) for count in counts],
        flops=2 * sum(counts) * width * latents,
        limit=16 + max(0, sum(counts) - 512) // 32,
    )


def last_body(
    cuts, groups, tile, all_rows, entries, energy_ref, own_ref, column_ref, row_ref, dec_ref, enc_sum, dec_sum,
    sums_ref, rows_ref, coded_ref, slope_ref, *refs,
):
    rows, grads, coded, parts = (refs[i * groups : (i + 1) * groups] for i in range(4))
    refs = refs[4 * groups :]
    count = len(cuts)
    pieces, (enc_out, dec_out, enc_buffer, dec_buffer, residual, part, sems) = refs[:count], refs[count:]
    columns = dec_buffer.shape[2]
    steps = dec_ref.shape[0] // tile
    scale = norm_scale(energy_ref, entries)
    join(pieces, residual, cuts)
    part[...] = own_columns(residual, own_ref, columns)

    def copies(step):
        slot, here = step % 2, pl.ds(step * tile, tile)
        return (
            pltpu.make_async_copy(enc_buffer.at[slot], enc_out.at[:, here], sems.at[slot, 0]),
            pltpu.make_async_copy(dec_buffer.at[slot], dec_out.at[here], sems.at[slot, 1]),
        )

    for step in range(steps):
        if step >= 2:
            for copy in copies(step - 2):
                copy.wait()
        here = slice(step * tile, (step + 1) * tile)
        enc, dec, sums = enc_sum[:, here], dec_sum[here, :], sums_ref[here, :]
        for coded_set, part_set in zip((*coded, coded_ref), (*parts, part), strict=True):
            dec = dec + jnp.dot(coded_set[here, :], part_set[...], preferred_element_type=jnp.float32)
            sums = sums + jnp.sum(coded_set[here, :].astype(jnp.float32), axis=1, keepdims=True)
        weights = own_columns(dec_ref.at[here, :], own_ref, columns).astype(jnp.float32)
        factor = sums / column_ref[here, :] * (sparsity_weight / all_rows)
        dec_buffer[step % 2] = dec * (2.0 / all_rows) + factor * weights
        copies(step)[1].start()
        for rows_set, grad in zip(rows, grads, strict=True):
            enc = enc + jnp.dot(rows_set[...], grad[:, here], preferred_element_type=jnp.float32)
        grad = pre_tile(residual, dec_ref, row_ref, slope_ref, here, all_rows)
        enc = enc + jnp.dot(rows_ref[...], grad, preferred_element_type=jnp.float32)
        enc_buffer[step % 2] = enc * scale
        copies(step)[0].start()
    for step in range(max(steps - 2, 0), steps):
        for copy in copies(step):
            copy.wait()


def weight_gradients(all_rows, entries, energy, own, column, row, dec, early, middle, encoded, pieces):
    coded, slope, rows = encoded
    columns = rows.shape[0]
    latents, width = dec.shape
    pieces, cuts = cut_pieces(pieces)
    count = sum(size for _, size in cuts)
    tile = min(512, latents)
    middle = [x for kind in zip(*middle, strict=True) for x in kind]
    args = [column, row, held(dec), *early, rows, coded, slope, *middle, *pieces]
    return kernel_call(
        functools.partial(last_body, cuts, len(middle) // 4, tile, all_rows, entries),
        [energy, own, *args],
        [IN_VMEM, IN_SMEM] + [IN_VMEM] * len(args),
        [pltpu.HBM((columns, latents), jnp.float32), pltpu.HBM((latents, columns), jnp.float32)],
        [
            pltpu.VMEM((2, columns, tile), jnp.float32),
            pltpu.VMEM((2, tile, columns), jnp.float32),
            pltpu.VMEM((count, width), jnp.bfloat16),
            pltpu.VMEM((count, columns), jnp.bfloat16),
            pltpu.SemaphoreType.DMA((2, 2)),
        ],
        [IN_HBM, IN_HBM],
        flops=2 * count * width * latents + 4 * count * columns * latents,
        limit=16,
    )


def bits(size):
    found, bit = [], 1
    while bit < size:
        found.append(bit)
        bit *= 2
    return found


def swap(x, even, odd=None):
    count = lax.axis_size("dp") * lax.axis_size("latent")
    odd = even if odd is None else odd
    return lax.ppermute(
        x, ("dp", "latent"), [(i, i ^ (odd if i & 1 else even)) for i in range(count)]
    )


def line_steps():
    steps = bits(lax.axis_size("latent"))[1:]
    return list(zip(steps[::-1], steps, strict=True))


def plane_steps():
    latent_size = lax.axis_size("latent")
    steps = [bit * latent_size for bit in bits(lax.axis_size("dp"))]
    return list(zip(steps, steps[::-1], strict=True))


def after(value, *done):
    return lax.optimization_barrier((value, *done))[0]


def after(value, *done):
    return lax.optimization_barrier((value, *done))[0]


def send_body(group_bits, own_ref, shuffle_ref, rows_ref, *outs):
    count, width = rows_ref.shape
    per_peer = outs[0].shape[0]
    goes_to = lax.shift_right_logical(shuffle_ref[...], group_bits) ^ own_ref[0]
    slot = shuffle_ref[...] & (count - 1)
    over_lanes = (((1,), (1,)), ((), ()))
    sublane = lax.broadcasted_iota(jnp.int32, (count, count), 0)
    lane = lax.broadcasted_iota(jnp.int32, (count, count), 1)
    peer_row = jnp.broadcast_to(goes_to, (count, count)).astype(jnp.float32)
    one_hot = (sublane == lane).astype(jnp.bfloat16)
    peer_column = lax.dot_general(
        one_hot, peer_row.astype(jnp.bfloat16), over_lanes, preferred_element_type=jnp.float32
    )
    before = (peer_column == peer_row) & (sublane < lane)
    rank = jnp.sum(before.astype(jnp.float32), axis=0, keepdims=True)
    order = goes_to.astype(jnp.float32) * per_peer + rank
    pick = (order == sublane.astype(jnp.float32)).astype(jnp.bfloat16)
    rows = jnp.dot(pick, rows_ref[...], preferred_element_type=jnp.float32)
    slot_rows = jnp.broadcast_to(slot, (128, count)).astype(jnp.float32).astype(jnp.bfloat16)
    slots = lax.dot_general(pick, slot_rows, over_lanes, preferred_element_type=jnp.float32)
    for peer, out in enumerate(outs):
        here = slice(peer * per_peer, (peer + 1) * per_peer)
        out[:, :width] = rows[here]
        out[:, width:] = slots[here]


def place_body(*refs):
    *pieces, out_ref, rows = refs
    join(pieces, rows)
    width = out_ref.shape[1]
    index = lax.broadcasted_iota(jnp.int32, (rows.shape[0], rows.shape[0]), 1).astype(jnp.float32)
    pick = (rows[:, width : width + 1] == index).astype(jnp.bfloat16)
    out_ref[...] = lax.dot_general(
        pick, rows[:, :width].astype(jnp.bfloat16), (((0,), (0,)), ((), ())), preferred_element_type=jnp.float32
    ).astype(jnp.bfloat16)


def send_rows(own, rows, shuffle):
    data_size = lax.axis_size("dp")
    latent_size = lax.axis_size("latent")
    count, width = rows.shape
    out = float_array(count // data_size, width + 128)
    body = functools.partial(send_body, len(bits(count * latent_size)))
    specs = [IN_SMEM, IN_VMEM, IN_VMEM]
    sent = kernel_call(body, [own, shuffle, rows], specs, [out] * data_size, limit=4)
    return [swap(x, peer * latent_size) if peer else x for peer, x in enumerate(sent)]


def place_rows(arrived, count, width):
    scratch = [pltpu.VMEM((count, width + 128), jnp.float32)]
    specs = [IN_VMEM] * len(arrived)
    return kernel_call(place_body, arrived, specs, [half_array(count, width)], scratch, limit=4)[0]


def shards(
    queries,
    cache_keys,
    cache_values,
    positions,
    shuffle,
    enc_weight,
    enc_bias,
    dec_weight,
    dec_bias,
):
    rows_here = queries.shape[0]
    att_width = queries.shape[1]
    data_size = lax.axis_size("dp")
    latent_size = lax.axis_size("latent")
    all_rows = rows_here * data_size * latent_size
    columns = att_width // data_size
    entries = all_rows * att_width
    core = (1, 1)
    line, plane = line_steps(), plane_steps()
    own = lax.axis_index("dp").astype(jnp.int32).reshape(1)
    bias, out_bias, places, own = lax.optimization_barrier(
        (enc_bias[None, :], dec_bias[None, :], shuffle[None, :], own)
    )
    heads_out, energy = attend(after(queries, bias, out_bias, places, own), cache_keys, cache_values, positions)

    small_steps = plane + [core] + line
    enc, latents_here = [], enc_weight.shape[1]
    rows = heads_out
    for number, mask in enumerate(line):
        arrived = swap(rows, *mask)
        count = len(plane) if number == 0 else 1
        if number == len(line) - 1:
            count = len(small_steps)
        for small in small_steps[:count]:
            other = swap(energy, *small)
            if small == line[0]:
                dec = load(after(dec_weight, energy), 0, att_width)
                other = after(other, dec)
            elif small in plane[:2]:
                side = latents_here // 2
                enc.append(load(after(enc_weight, energy), len(enc) * side, side))
                other = after(other, enc[-1])
            energy = add(energy, other)
        small_steps = small_steps[count:]
        rows = joined(rows, after(arrived, energy))
        if number == 0:
            pair = rows

    def chunks(near, far, first, size, largest=256):
        step = min(size, largest)
        return [[(near, i, step), (far, i, step)] for i in range(first, first + size, step)]

    hop = swap(rows, *plane[0])
    group = whole([rows, swap(rows, *core)])
    *first_set, keep, send = encode_and_rebuild(entries, energy, own, enc, bias, dec, group, columns)
    encoded = [first_set]

    def encode_next(parts, now):
        parts = [(after(part, now), *cut) for part, *cut in parts]
        encoded.append(encode(entries, energy, own, enc, bias, parts, columns))
        return encoded[-1][0]

    arrived = swap(send, *core)
    total = after(keep, hop)
    far = [rows, hop]
    for number, mask in enumerate(line[::-1]):
        last = number == len(line) - 1
        total, sent = (add_both if last else add_split)(total, arrived)
        arrived = swap(sent, *mask)
        if number == 0:
            hop = after(hop, sent)
            arrived = after(arrived, encode_next(whole([hop, swap(hop, *core)]), sent))
            for step in plane[1:2]:
                far.append(swap(joined(*(after(piece, sent) for piece in far), halves=True), *step))
        if last:
            norms_column, norms_row = decoder_norms(after(dec, sent))
            arrived = after(arrived, norms_row, far[-1])
    rebuilt_own, rows = pair_residual(entries, total, arrived, out_bias, pair, energy)
    for step in plane[2:]:
        far.append(swap(joined(*(after(piece, rows) for piece in far), halves=True), *step))
    others = [swap(after(piece, rows), *core) for piece in far[2:]]

    for mask in line[1:-1]:
        rows = joined(rows, swap(rows, *mask))
    near, late = [rows], [swap(rows, *line[-1])]
    near.append(swap(rows, *plane[0]))
    moved = send_rows(own, after(rebuilt_own, rows), places)
    waiting = []
    for piece, other in zip(far[2:], others, strict=True):
        half = piece.shape[0] // 2
        waiting += chunks(piece, other, 0, half) + chunks(piece, other, half, half)
    done = [encode_next(parts, rows) for parts in waiting[:-1]]
    late[0] = after(late[0], near[1], *done, *moved)
    grads = []

    def pre(sets, now):
        slopes = [code[1] for code in encoded[len(grads) : len(grads) + len(sets)]]
        sets = [[(after(part, now), *cut) for part, *cut in parts] for parts in sets]
        grads.extend(pre_gradient(all_rows, own, dec, norms_row, slopes, sets, columns))
        return grads[-1][0]

    def ready(sets):
        chosen = [(encoded[i], grads[i]) for i in sets]
        return [(code[2], grad[0], code[0], grad[1]) for code, grad in chosen]

    late.append(swap(late[0], *plane[0]))
    near.append(swap(joined(*near), *plane[1]))
    rows = joined(near[0], late[0])
    done = pre([whole([rows, swap(rows, *core)])], rows)
    near[2] = after(near[2], done)
    hop = joined(near[1], after(late[1], done, encode_next(waiting[-1], rows)))
    sets = [whole([hop, swap(hop, *core)])]
    for number, step in enumerate(plane[1:], 1):
        if number > 1:
            near.append(swap(joined(*near), *step))
        late.append(swap(joined(*late), *step))
        sets += chunks(near[-1], swap(near[-1], *core), 0, near[-1].shape[0])
        if number < len(plane) - 1:
            sets += chunks(late[-1], swap(late[-1], *core), 0, late[-1].shape[0])
    for first in range(0, len(sets) - 2, 2):
        done = pre(sets[first : first + 2], hop)
    count = len(grads)
    sets = [[(after(part, hop), *cut) for part, *cut in parts] for parts in sets[count - 1 :]]
    early = early_sums(all_rows, own, dec, norms_row, encoded[: count + len(sets)], grads, sets)
    count += len(sets)
    grads += [None] * len(sets)
    last = after(late[-1], early[0])
    sets = chunks(last, swap(last, *core), 0, last.shape[0])
    for parts in sets[:-1]:
        pre([parts], last)
    grad_enc, grad_dec = weight_gradients(
        all_rows,
        entries,
        energy,
        own,
        norms_column,
        norms_row,
        dec,
        early,
        ready(range(count, len(grads))),
        encoded[-1],
        sets[-1],
    )
    rebuilt = place_rows([after(part, early[0]) for part in moved], rows_here, att_width)
    return (rebuilt, grad_enc, grad_dec)


def solution(mesh):
    in_specs = (
        P(("dp", "latent"), None),
        P(("dp", "latent"), None, None),
        P(("dp", "latent"), None, None),
        P(("dp", "latent")),
        P(("dp", "latent")),
        P(None, "latent"),
        P("latent"),
        P("latent", None),
        P(),
    )
    out_specs = (P(("dp", "latent"), None), P("dp", "latent"), P("latent", "dp"))
    return jax.shard_map(shards, mesh=mesh, in_specs=in_specs, out_specs=out_specs, check_vma=False)
```
